32 devices in a mesh: groups: 2 (over x), ctx: 16 (over z, y, core).
Axes of the slice: x: 2, y: 2, z: 4, core: 2. Of those that a mesh axis runs over, the one named last changes fastest.
Arguments:
- src_cache: bfloat16 [1024, 2, 2, 16, 1024], P(('groups', 'ctx')), parts along dimension 0, may hold values from -6 to 6
- src_blocks: int32 [1024], P('groups'), parts along dimension 0, may hold values from 0 to 511, as said below
- dst_blocks: int32 [1024], P('groups'), parts along dimension 0, may hold values from 0 to 511, as said below
- ctx_lengths: int32 [8], P('groups'), parts along dimension 0, may hold values from 1024 to 2048, as said below
- queries: bfloat16 [5, 2, 8, 16384], P(None, None, 'groups'), parts along dimension 2, may hold values from -120 to 120
- new_keys: bfloat16 [5, 2, 8, 1024], P(None, None, 'groups'), parts along dimension 2, may hold values from -16 to 16
- new_values: bfloat16 [5, 2, 8, 1024], P(None, None, 'groups'), parts along dimension 2, may hold values from -6 to 6
Outputs:
- dst_cache: bfloat16 [1024, 2, 2, 16, 1024], P(('groups', 'ctx')), parts along dimension 0
- attn_out: float32 [5, 2, 1024, 128], P(None, None, ('groups', 'ctx')), parts along dimension 2
The draws below stay inside these ranges and needn't reach their ends.
There are 2 independent parts, one for each index of `groups`. The reference program is written for one: setup_inputs(seed, part) draws one part's arguments, and reference() takes and returns one part's arrays. A program takes and returns all parts, laid end to end along the dimension named above; each array names one. Nothing has to cross between parts.
Inputs may be any that keep to these rules, and one draw needn't show every extreme that they name: `src_blocks`: A permutation of the blocks; device k of ctx holds source slots k * 32 to (k + 1) * 32 - 1. `dst_blocks`: A permutation of the blocks; device k of ctx holds destination slots k * 32 to (k + 1) * 32 - 1. At most 2 blocks goes from the source slots of one device to the destination slots of one device, and some pair of devices has exactly 2. `ctx_lengths`: some request has exactly 2048 cached tokens.
All inputs are finite; a program needn't handle non-finite values.
Results may differ from the reference program's by a relative error of at most 0.001.
Values may be sent and summed in bfloat16 or wider, within the bound.
A program may use at most 256 MiB of HBM per device.

```python
import jax
import jax.numpy as jnp
from jax import lax

KVH = 8
HD = 128
QPG = 16
LAYERS = 2
REQS = 4
STEPS = 4
BLK = 16
BLK_DEV = 32
NBLK = 512
CTXLEN = 2048
CAP = 2
QH = 128
KVW = 1024


def block_tables(key):
    base = jax.random.fold_in(key, 11)
    perm_key, shift_key, dest_key = jax.random.split(base, 3)
    device_count = NBLK // BLK_DEV
    src_blocks = jax.random.permutation(perm_key, NBLK).astype(jnp.int32)
    shuffled = jax.random.permutation(shift_key, device_count).astype(jnp.int32)
    place_of = jnp.zeros((device_count,), jnp.int32).at[shuffled].set(jnp.arange(device_count, dtype=jnp.int32))
    device_ids = jnp.arange(device_count, dtype=jnp.int32)
    scores = jnp.where(device_ids == device_count // 2, 0, jnp.where(device_ids == 1, 1, place_of + 2)).astype(jnp.int32)
    order = jnp.argsort(scores, stable=True).astype(jnp.int32)
    shifts = jnp.tile(order, CAP)[:BLK_DEV]
    arrange = jax.vmap(lambda sub_key: jax.random.permutation(sub_key, BLK_DEV))(jax.random.split(dest_key, device_count)).astype(jnp.int32)
    target_dev = jnp.arange(device_count, dtype=jnp.int32)[:, None]
    slot_pos = jnp.arange(BLK_DEV, dtype=jnp.int32)[None, :]
    source_slot = (target_dev - shifts[None, :]) % device_count * BLK_DEV + slot_pos
    dest_slot = target_dev * BLK_DEV + arrange
    dst_blocks = jnp.zeros((NBLK,), jnp.int32).at[dest_slot.reshape(-1)].set(src_blocks[source_slot].reshape(-1))
    return (src_blocks, dst_blocks)


def draw_src_blocks(key, part):
    return block_tables(key)[0]


def draw_dst_blocks(key, part):
    return block_tables(key)[1]


def draw_ctx_lengths(key, part):
    base = jax.random.fold_in(key, 23)
    len_key, pick_key = jax.random.split(base)
    lengths = jax.random.randint(len_key, (REQS,), CTXLEN // 2, CTXLEN + 1).astype(jnp.int32)
    chosen = jax.random.randint(pick_key, (), 0, REQS)
    return lengths.at[chosen].set(CTXLEN).astype(jnp.int32)


def draw_src_cache(key, part):
    cache = jnp.clip(jax.random.normal(jax.random.fold_in(key, 5), (NBLK, LAYERS, 2, BLK, KVW), jnp.float32), -6.0, 6.0)
    return cache.astype(jnp.bfloat16)


def draw_queries(key, part):
    shape = (STEPS + 1, LAYERS, REQS, KVH, QPG, HD)
    base = jnp.clip(jax.random.normal(jax.random.fold_in(key, 7), shape, jnp.float32), -6.0, 6.0)
    base = jnp.clip(base, -120.0, 120.0)
    return base.reshape(STEPS + 1, LAYERS, REQS, QH * HD).astype(jnp.bfloat16)


def noise(own_key, shape, width, reach, kind=jnp.bfloat16):
    return jnp.clip(width * jax.random.normal(own_key, shape, jnp.float32), -reach, reach).astype(kind)


def setup_inputs(seed: int = 0, part: int = 0) -> dict:
    seeds = jax.random.split(jax.random.key(seed), 8)
    own_keys = jax.random.split(jax.random.fold_in(seeds[7], part), 8)
    src_cache = draw_src_cache(jax.random.fold_in(jax.random.fold_in(seeds[7], part), 71), part)
    src_blocks = draw_src_blocks(jax.random.fold_in(jax.random.fold_in(seeds[7], part), 71), part)
    dst_blocks = draw_dst_blocks(jax.random.fold_in(jax.random.fold_in(seeds[7], part), 71), part)
    ctx_lengths = draw_ctx_lengths(jax.random.fold_in(jax.random.fold_in(seeds[7], part), 71), part)
    queries = draw_queries(jax.random.fold_in(jax.random.fold_in(seeds[7], part), 71), part)
    new_keys = noise(own_keys[5], (STEPS + 1, LAYERS, REQS, KVW), 4.0, 16.0)
    new_values = noise(own_keys[6], (STEPS + 1, LAYERS, REQS, KVW), 1.0, 6.0)
    return dict(src_cache=src_cache, src_blocks=src_blocks, dst_blocks=dst_blocks, ctx_lengths=ctx_lengths, queries=queries, new_keys=new_keys, new_values=new_values)


def reference(src_cache, src_blocks, dst_blocks, ctx_lengths, queries, new_keys, new_values):
    block_total = src_blocks.shape[0]
    slot_ids = jnp.arange(block_total, dtype=jnp.int32)
    inv_src = jnp.zeros((block_total,), jnp.int32).at[src_blocks].set(slot_ids)
    dst_cache = jnp.take(src_cache, inv_src[dst_blocks], axis=0)
    per_request = block_total // REQS
    ordered = jnp.take(src_cache, inv_src, axis=0)
    ordered = ordered.reshape(REQS, per_request, LAYERS, 2, BLK, KVH, HD)
    ordered = jnp.transpose(ordered, (2, 3, 0, 1, 4, 5, 6)).reshape(LAYERS, 2, REQS, CTXLEN, KVH, HD)
    positions = jnp.arange(CTXLEN, dtype=jnp.int32)
    in_context = positions[None, :] < ctx_lengths[:, None]
    score_scale = HD ** -0.5
    highest = lax.Precision.HIGHEST
    results = []
    for step_idx in range(STEPS + 1):
        per_layer = []
        for layer_idx in range(LAYERS):
            query_heads = queries[step_idx, layer_idx].reshape(REQS, KVH, QPG, HD).astype(jnp.float32)
            cache_keys = ordered[layer_idx, 0].astype(jnp.float32)
            cache_scores = jnp.einsum('rkgd,rtkd->rkgt', query_heads, cache_keys, precision=highest) * score_scale
            cache_scores = jnp.where(in_context[:, None, None, :], cache_scores, -jnp.inf)
            fresh_keys = new_keys[:step_idx + 1, layer_idx].reshape(step_idx + 1, REQS, KVH, HD).astype(jnp.float32)
            fresh_scores = jnp.einsum('rkgd,srkd->rkgs', query_heads, fresh_keys, precision=highest) * score_scale
            row_max = jnp.maximum(jnp.max(cache_scores, axis=-1), jnp.max(fresh_scores, axis=-1))
            cache_weights = jnp.exp(cache_scores - row_max[..., None])
            fresh_weights = jnp.exp(fresh_scores - row_max[..., None])
            totals = jnp.sum(cache_weights, axis=-1) + jnp.sum(fresh_weights, axis=-1)
            fresh_vals = new_values[:step_idx + 1, layer_idx].reshape(step_idx + 1, REQS, KVH, HD).astype(jnp.float32)
            weighted = jnp.einsum('rkgt,rtkd->rkgd', cache_weights, ordered[layer_idx, 1].astype(jnp.float32), precision=highest)
            weighted = weighted + jnp.einsum('rkgs,srkd->rkgd', fresh_weights, fresh_vals, precision=highest)
            per_layer.append((weighted / totals[..., None]).reshape(REQS * QH, HD))
        results.append(jnp.stack(per_layer))
    return dst_cache, jnp.stack(results)
```

```python
import functools

import jax
import jax.numpy as jnp
from jax import lax
from jax.experimental import pallas as pl
from jax.experimental.pallas import tpu as pltpu
from jax.sharding import PartitionSpec as P

KVH = 8
HD = 128
QPG = 16
REQS = 4

NEG_BIG = -1e30
STAT_ROWS = 8
MESH = pl.DeviceIdType.MESH


def move_blocks(index_ref, src_ref, out_ref, sems):
    count = out_ref.shape[0]

    def copy(i):
        return pltpu.make_async_copy(src_ref.at[index_ref[i]], out_ref.at[i], sems.at[i])

    lax.fori_loop(0, count, lambda i, c: (copy(i).start(), c)[1], 0)
    lax.fori_loop(0, count, lambda i, c: (copy(i).wait(), c)[1], 0)


def take_blocks(src, index):
    count = index.shape[0]
    return pl.pallas_call(
        move_blocks,
        out_shape=jax.ShapeDtypeStruct((count,) + src.shape[1:], src.dtype),
        in_specs=[
            pl.BlockSpec(memory_space=pltpu.SMEM),
            pl.BlockSpec(memory_space=pl.ANY),
        ],
        out_specs=pl.BlockSpec(memory_space=pl.ANY),
        scratch_shapes=[pltpu.SemaphoreType.DMA((count,))],
        name="take_blocks",
    )(index, src)


def split_bf16(value):
    high = value.astype(jnp.bfloat16)
    low = (value - high.astype(jnp.float32)).astype(jnp.bfloat16)
    return high, low


def dot(a, b, b_dim):
    return lax.dot_general(
        a, b, (((1,), (b_dim,)), ((), ())), preferred_element_type=jnp.float32
    )


def exchange_kernel(
    n,
    groups,
    halves,
    out_blocks,
    cache,
    queries,
    fresh_keys,
    fresh_values,
    token_request,
    fresh_bias,
    arrived,
    result,
    acc,
    acc_in,
    stat,
    stat_in,
    stat_cols,
    block_send,
    block_recv,
    acc_send,
    acc_recv,
    stat_send,
    stat_recv,
    own_sems,
):
    me = lax.axis_index("ctx")
    blocks, layers, _, block_len, _ = cache.shape
    tokens = blocks * block_len
    rows = acc.shape[3]
    width = rows * halves

    def peer(k):
        return lax.rem(me + k, n)

    def each(body):
        lax.fori_loop(1, n, lambda k, c: (body(k), c)[1], 0)

    barrier = pltpu.get_barrier_semaphore()
    each(lambda k: pl.semaphore_signal(barrier, 1, device_id={"ctx": peer(k)}, device_id_type=MESH))
    pl.semaphore_wait(barrier, n - 1)

    def remote(src, dst, send, recv, k):
        return pltpu.make_async_remote_copy(
            src_ref=src.at[peer(k)],
            dst_ref=dst.at[me],
            send_sem=send.at[k],
            recv_sem=recv.at[k],
            device_id={"ctx": peer(k)},
            device_id_type=MESH,
        )

    def block_copy(k):
        return remote(out_blocks, arrived, block_send, block_recv, k)

    def acc_copy(k):
        return remote(acc, acc_in, acc_send, acc_recv, k)

    def stat_copy(k):
        return remote(stat, stat_in, stat_send, stat_recv, k)

    each(lambda k: block_copy(k).start())
    own_blocks = pltpu.make_async_copy(out_blocks.at[me], arrived.at[me], own_sems.at[0])
    own_blocks.start()

    stat_cols[...] = jnp.zeros_like(stat_cols)
    lane = lax.broadcasted_iota(jnp.int32, (1, HD), 1)
    fresh_live = jnp.where(me == 0, 0.0, NEG_BIG)

    def head(g, carry):
        cols = pl.ds(pl.multiple_of(g * HD, HD), HD)
        for layer in range(layers):
            q = queries[layer, g]
            k_cache = cache[:, layer, 0, :, cols].reshape(tokens, HD)
            v_cache = cache[:, layer, 1, :, cols].reshape(tokens, HD)
            k_new = fresh_keys[layer, :, cols]
            v_new = fresh_values[layer, :, cols]
            scores = dot(q, k_cache, 1) * (HD**-0.5)
            new_scores = dot(q, k_new, 1) * (HD**-0.5)
            for r in range(REQS):
                part = slice(r * width, (r + 1) * width)
                live = jnp.where(token_request[...] == r, 0.0, NEG_BIG)
                s = scores[part] + live
                s_new = new_scores[part] + (fresh_bias[part] + fresh_live)
                top = jnp.maximum(
                    jnp.max(s, axis=1, keepdims=True), jnp.max(s_new, axis=1, keepdims=True)
                )
                w = jnp.exp(s - top)
                w_new = jnp.exp(s_new - top)
                total = jnp.sum(w, axis=1, keepdims=True) + jnp.sum(w_new, axis=1, keepdims=True)
                high, low = split_bf16(w)
                new_high, new_low = split_bf16(w_new)
                sums = (
                    dot(high, v_cache, 0)
                    + dot(low, v_cache, 0)
                    + dot(new_high, v_new, 0)
                    + dot(new_low, v_new, 0)
                )
                for h in range(halves):
                    chunk = (r * KVH + g) * halves + h
                    acc[chunk // groups, chunk % groups, layer] = sums[h * rows : (h + 1) * rows]
                at = g * STAT_ROWS + layer
                now = stat_cols[part]
                now = jnp.where(lane == at, top, now)
                stat_cols[part] = jnp.where(lane == at + layers, total, now)
        return carry

    lax.fori_loop(0, KVH, head, 0)

    pad = jnp.zeros((HD - rows, HD), jnp.float32)
    for r in range(REQS):
        for h in range(halves):
            start = (r * halves + h) * rows
            turned = jnp.concatenate([stat_cols[start : start + rows], pad], axis=0).T
            for g in range(KVH):
                chunk = (r * KVH + g) * halves + h
                stat[chunk // groups, chunk % groups] = turned[
                    g * STAT_ROWS : (g + 1) * STAT_ROWS
                ]

    each(lambda k: (stat_copy(k).start(), acc_copy(k).start()))
    own_acc = pltpu.make_async_copy(acc.at[me], acc_in.at[me], own_sems.at[1])
    own_stat = pltpu.make_async_copy(stat.at[me], stat_in.at[me], own_sems.at[2])
    own_acc.start()
    own_stat.start()
    own_acc.wait()
    own_stat.wait()
    each(lambda k: (stat_copy(k).wait(), acc_copy(k).wait()))

    share = rows // result.shape[0]
    for gi in range(groups):
        for layer in range(layers):
            tops = stat_in[:, gi, layer, :]
            top = jnp.max(tops, axis=0, keepdims=True)
            factor = jnp.exp(tops - top)
            total = jnp.sum(factor * stat_in[:, gi, layers + layer, :], axis=0, keepdims=True)
            factor = factor / total
            factor = jnp.concatenate([factor, jnp.zeros((HD - n, HD), jnp.float32)], axis=0).T
            out = jnp.zeros((rows, HD), jnp.float32)
            for src in range(n):
                out = out + factor[:rows, src : src + 1] * acc_in[src, gi, layer]
            for step in range(result.shape[0]):
                result[step, layer, gi * share : (gi + 1) * share, :] = out[
                    step * share : (step + 1) * share
                ]

    own_blocks.wait()
    each(lambda k: block_copy(k).wait())


def exchange(n, outgoing, cache, queries, fresh_keys, fresh_values, token_request):
    steps, layers, requests, _ = queries.shape
    share = requests * KVH * QPG // n
    groups = max(share // QPG, 1)
    halves = max(QPG // share, 1)
    heads = QPG // halves
    rows = steps * heads
    q = queries.reshape(steps, layers, requests, KVH, halves, heads, HD)
    q = jnp.transpose(q, (1, 3, 2, 4, 0, 5, 6)).reshape(
        layers, KVH, requests * halves * rows, HD
    )
    fresh = steps * requests
    fresh_pad = -(-fresh // 16) * 16

    def fresh_rows(value):
        value = jnp.transpose(value, (1, 0, 2, 3)).reshape(layers, fresh, KVH * HD)
        return jnp.pad(value, ((0, 0), (0, fresh_pad - fresh), (0, 0)))

    row = jnp.arange(requests * halves * rows)
    row_request = row // (halves * rows)
    row_step = row % rows // heads
    col = jnp.arange(fresh_pad)
    seen = (
        (col[None, :] % requests == row_request[:, None])
        & (col[None, :] // requests <= row_step[:, None])
        & (col[None, :] < fresh)
    )
    fresh_bias = jnp.where(seen, 0.0, NEG_BIG).astype(jnp.float32)
    vmem = pl.BlockSpec(memory_space=pltpu.VMEM)
    hbm = pl.BlockSpec(memory_space=pl.ANY)
    dma = pltpu.SemaphoreType.DMA
    return pl.pallas_call(
        functools.partial(exchange_kernel, n, groups, halves),
        out_shape=(
            jax.ShapeDtypeStruct(outgoing.shape, outgoing.dtype),
            jax.ShapeDtypeStruct((steps, layers, share, HD), jnp.float32),
        ),
        in_specs=[hbm] + [vmem] * 6,
        out_specs=(hbm, vmem),
        scratch_shapes=[
            pltpu.VMEM((n, groups, layers, rows, HD), jnp.float32),
            pltpu.VMEM((n, groups, layers, rows, HD), jnp.float32),
            pltpu.VMEM((n, groups, STAT_ROWS, HD), jnp.float32),
            pltpu.VMEM((n, groups, STAT_ROWS, HD), jnp.float32),
            pltpu.VMEM((requests * halves * rows, HD), jnp.float32),
            dma((n,)),
            dma((n,)),
            dma((n,)),
            dma((n,)),
            dma((n,)),
            dma((n,)),
            dma((3,)),
        ],
        compiler_params=pltpu.CompilerParams(
            collective_id=0, has_side_effects=True, vmem_limit_bytes=48 * 1024 * 1024
        ),
        name="exchange",
    )(outgoing, cache, q, fresh_rows(fresh_keys), fresh_rows(fresh_values), token_request, fresh_bias)


def local(src_cache, src_blocks, dst_blocks, ctx_lengths, queries, new_keys, new_values):
    n = lax.axis_size("ctx")
    me = lax.axis_index("ctx")
    per_dev, _, _, block_len, _ = src_cache.shape
    total = src_blocks.shape[0]
    per_request = total // REQS
    cap = (per_dev + n - 1) // n
    slots = jnp.arange(total, dtype=jnp.int32)
    pos = jnp.arange(per_dev, dtype=jnp.int32)
    src_ids = lax.dynamic_slice_in_dim(src_blocks, me * per_dev, per_dev)
    dst_ids = lax.dynamic_slice_in_dim(dst_blocks, me * per_dev, per_dev)

    target = jnp.sum(jnp.where(src_ids[:, None] == dst_blocks[None], slots[None], 0), axis=1) // per_dev
    before = (target[:, None] == target[None]) & (pos[None] < pos[:, None])
    bucket = target * cap + jnp.sum(before.astype(jnp.int32), axis=1)
    bucket_ids = jnp.arange(n * cap, dtype=jnp.int32)
    chosen = jnp.sum(jnp.where(bucket_ids[:, None] == bucket[None], pos[None], 0), axis=1)

    root = jnp.sum(jnp.where(dst_ids[:, None] == src_blocks[None], slots[None], 0), axis=1)
    owner = root // per_dev
    earlier = (owner[:, None] == owner[None]) & (root[None] < root[:, None])
    rows = owner * cap + jnp.sum(earlier.astype(jnp.int32), axis=1)

    request = src_ids // per_request
    limit = jnp.sum(
        jnp.where(request[:, None] == jnp.arange(REQS)[None], ctx_lengths[None], 0), axis=1
    )
    at = (src_ids % per_request)[:, None] * block_len + jnp.arange(block_len)[None]
    token_request = jnp.where(at < limit[:, None], request[:, None], -1).astype(jnp.int32)
    token_request = token_request.reshape(1, per_dev * block_len)

    outgoing = take_blocks(src_cache, chosen)
    outgoing = outgoing.reshape((n, cap) + src_cache.shape[1:])
    arrived, attn = exchange(
        n, outgoing, src_cache, queries, new_keys, new_values, token_request
    )
    dst_cache = take_blocks(arrived.reshape((n * cap,) + src_cache.shape[1:]), rows)
    return dst_cache, attn


def solution(mesh):
    in_specs = (
        P(("groups", "ctx"), None, None, None, None),
        P("groups"),
        P("groups"),
        P("groups"),
        P(None, None, "groups", None),
        P(None, None, "groups", None),
        P(None, None, "groups", None),
    )
    out_specs = (
        P(("groups", "ctx"), None, None, None, None),
        P(None, None, ("groups", "ctx"), None),
    )
    return jax.shard_map(local, mesh=mesh, in_specs=in_specs, out_specs=out_specs, check_vma=False)
```

```python
import functools

import jax
import jax.numpy as jnp
from jax import lax
from jax.experimental import pallas as pl
from jax.experimental.pallas import tpu as pltpu
from jax.sharding import PartitionSpec as P

KVH = 8
HD = 128
QPG = 16
REQS = 4

NEG_BIG = -1e30
STAT_ROWS = 8
MESH = pl.DeviceIdType.MESH


def split_bf16(value):
    high = value.astype(jnp.bfloat16)
    low = (value - high.astype(jnp.float32)).astype(jnp.bfloat16)
    return high, low


def dot(a, b, b_dim):
    return lax.dot_general(
        a, b, (((1,), (b_dim,)), ((), ())), preferred_element_type=jnp.float32
    )


def exchange_kernel(
    n,
    groups,
    halves,
    send_index,
    take_index,
    cache,
    queries,
    fresh_keys,
    fresh_values,
    token_request,
    fresh_bias,
    placed,
    result,
    outgoing,
    arrived,
    acc,
    acc_core,
    acc_near,
    acc_far,
    stat,
    stat_core,
    stat_near,
    stat_far,
    stat_cols,
    block_send,
    block_recv,
    pair_send,
    pair_recv,
    far_send,
    far_recv,
):
    me = lax.axis_index("ctx")
    blocks, layers, _, block_len, _ = cache.shape
    tokens = blocks * block_len
    cap = outgoing.shape[1]
    quarter = n // 4
    rows = acc.shape[5]
    width = rows * halves
    bit0 = lax.rem(me, 2)
    bit1 = lax.rem(me // 2, 2)
    high = me // 4

    def loop(start, stop, body):
        lax.fori_loop(start, stop, lambda k, c: (body(k), c)[1], 0)

    def peer(k):
        return lax.rem(me + k, n)

    def send(src, dst, send_sem, recv_sem, device):
        return pltpu.make_async_remote_copy(
            src_ref=src,
            dst_ref=dst,
            send_sem=send_sem,
            recv_sem=recv_sem,
            device_id={"ctx": device},
            device_id_type=MESH,
        )

    barrier = pltpu.get_barrier_semaphore()
    loop(
        1,
        n,
        lambda k: pl.semaphore_signal(
            barrier, 1, device_id={"ctx": peer(k)}, device_id_type=MESH
        ),
    )
    pl.semaphore_wait(barrier, n - 1)

    def block_copy(k):
        return send(
            outgoing.at[peer(k)], arrived.at[me], block_send.at[k], block_recv.at[k], peer(k)
        )

    def send_blocks(k):
        for c in range(cap):
            outgoing[peer(k), c] = cache[send_index[peer(k) * cap + c]]
        block_copy(k).start()

    loop(1, n, send_blocks)
    for c in range(cap):
        arrived[me, c] = cache[send_index[me * cap + c]]

    stat_cols[...] = jnp.zeros_like(stat_cols)
    lane = lax.broadcasted_iota(jnp.int32, (1, HD), 1)
    fresh_live = jnp.where(me == 0, 0.0, NEG_BIG)

    def head(g):
        cols = pl.ds(pl.multiple_of(g * HD, HD), HD)
        for layer in range(layers):
            q = queries[layer, g]
            k_cache = cache[:, layer, 0, :, cols].reshape(tokens, HD)
            v_cache = cache[:, layer, 1, :, cols].reshape(tokens, HD)
            k_new = fresh_keys[layer, :, cols]
            v_new = fresh_values[layer, :, cols]
            scores = dot(q, k_cache, 1) * (HD**-0.5)
            new_scores = dot(q, k_new, 1) * (HD**-0.5)
            for r in range(REQS):
                part = slice(r * width, (r + 1) * width)
                live = jnp.where(token_request[...] == r, 0.0, NEG_BIG)
                s = scores[part] + live
                s_new = new_scores[part] + (fresh_bias[part] + fresh_live)
                top = jnp.maximum(
                    jnp.max(s, axis=1, keepdims=True), jnp.max(s_new, axis=1, keepdims=True)
                )
                w = jnp.exp(s - top)
                w_new = jnp.exp(s_new - top)
                total = jnp.sum(w, axis=1, keepdims=True) + jnp.sum(w_new, axis=1, keepdims=True)
                big, small = split_bf16(w)
                new_big, new_small = split_bf16(w_new)
                sums = (
                    dot(big, v_cache, 0)
                    + dot(small, v_cache, 0)
                    + dot(new_big, v_new, 0)
                    + dot(new_small, v_new, 0)
                )
                for h in range(halves):
                    chunk = (r * KVH + g) * halves + h
                    to, gi = chunk // groups, chunk % groups
                    acc[to % 2, to // 2 % 2, to // 4, gi, layer] = sums[h * rows : (h + 1) * rows]
                at = g * STAT_ROWS + layer
                now = stat_cols[part]
                now = jnp.where(lane == at, top, now)
                stat_cols[part] = jnp.where(lane == at + layers, total, now)

    loop(0, KVH, head)

    pad = jnp.zeros((HD - rows, HD), jnp.float32)
    for r in range(REQS):
        for h in range(halves):
            start = (r * halves + h) * rows
            turned = jnp.concatenate([stat_cols[start : start + rows], pad], axis=0).T
            for g in range(KVH):
                chunk = (r * KVH + g) * halves + h
                to, gi = chunk // groups, chunk % groups
                stat[to % 2, to // 2 % 2, to // 4, gi] = turned[
                    g * STAT_ROWS : (g + 1) * STAT_ROWS
                ]

    def columns(factors):
        filler = jnp.zeros((HD - factors.shape[0], HD), jnp.float32)
        return jnp.concatenate([factors, filler], axis=0).T

    def join(acc_own, stat_own, acc_new, stat_new):
        for gi in range(groups):
            a, b = stat_own[gi], stat_new[gi]
            top = jnp.maximum(a[:layers], b[:layers])
            keep = jnp.exp(a[:layers] - top)
            add = jnp.exp(b[:layers] - top)
            total = a[layers : 2 * layers] * keep + b[layers : 2 * layers] * add
            filler = jnp.zeros((STAT_ROWS - 2 * layers, HD), jnp.float32)
            stat_own[gi] = jnp.concatenate([top, total, filler], axis=0)
            factor = columns(jnp.concatenate([keep, add], axis=0))
            for layer in range(layers):
                acc_own[gi, layer] = (
                    acc_own[gi, layer] * factor[:rows, layer : layer + 1]
                    + acc_new[gi, layer] * factor[:rows, layers + layer : layers + layer + 1]
                )

    def swap(copies):
        for copy in copies:
            copy.start()
        for copy in copies:
            copy.wait()

    core = me + 1 - 2 * bit0
    swap(
        [
            send(stat.at[1 - bit0], stat_core, pair_send.at[0], pair_recv.at[0], core),
            send(acc.at[1 - bit0], acc_core, pair_send.at[1], pair_recv.at[1], core),
        ]
    )

    def join_core(i):
        b, z = i // quarter, lax.rem(i, quarter)
        join(
            acc.at[bit0, b, z], stat.at[bit0, b, z], acc_core.at[b, z], stat_core.at[b, z]
        )

    loop(0, 2 * quarter, join_core)

    near = me + 2 - 4 * bit1
    swap(
        [
            send(stat.at[bit0, 1 - bit1], stat_near, pair_send.at[2], pair_recv.at[2], near),
            send(acc.at[bit0, 1 - bit1], acc_near, pair_send.at[3], pair_recv.at[3], near),
        ]
    )
    loop(
        0,
        quarter,
        lambda z: join(
            acc.at[bit0, bit1, z], stat.at[bit0, bit1, z], acc_near.at[z], stat_near.at[z]
        ),
    )

    def far_copies(k):
        to = lax.rem(high + k, quarter)
        device = to * 4 + lax.rem(me, 4)
        return (
            send(
                stat.at[bit0, bit1, to],
                stat_far.at[high],
                far_send.at[0, k],
                far_recv.at[0, k],
                device,
            ),
            send(
                acc.at[bit0, bit1, to], acc_far.at[high], far_send.at[1, k], far_recv.at[1, k], device
            ),
        )

    loop(1, quarter, lambda k: [copy.start() for copy in far_copies(k)])
    stat_far[high] = stat[bit0, bit1, high]
    acc_far[high] = acc[bit0, bit1, high]
    loop(1, quarter, lambda k: [copy.wait() for copy in far_copies(k)])

    share = rows // result.shape[0]
    for gi in range(groups):
        for layer in range(layers):
            tops = stat_far[:, gi, layer, :]
            top = jnp.max(tops, axis=0, keepdims=True)
            factor = jnp.exp(tops - top)
            total = jnp.sum(factor * stat_far[:, gi, layers + layer, :], axis=0, keepdims=True)
            factor = columns(factor / total)
            out = jnp.zeros((rows, HD), jnp.float32)
            for src in range(quarter):
                out = out + factor[:rows, src : src + 1] * acc_far[src, gi, layer]
            for step in range(result.shape[0]):
                result[step, layer, gi * share : (gi + 1) * share, :] = out[
                    step * share : (step + 1) * share
                ]

    loop(1, n, lambda k: block_copy(k).wait())

    def place(j):
        at = take_index[j]
        placed[j] = arrived[at // cap, lax.rem(at, cap)]

    loop(0, blocks, place)


def exchange(n, cap, send_index, take_index, cache, queries, fresh_keys, fresh_values, token_request):
    steps, layers, requests, _ = queries.shape
    share = requests * KVH * QPG // n
    groups = max(share // QPG, 1)
    halves = max(QPG // share, 1)
    heads = QPG // halves
    rows = steps * heads
    q = queries.reshape(steps, layers, requests, KVH, halves, heads, HD)
    q = jnp.transpose(q, (1, 3, 2, 4, 0, 5, 6)).reshape(
        layers, KVH, requests * halves * rows, HD
    )
    fresh = steps * requests
    fresh_pad = -(-fresh // 16) * 16

    def fresh_rows(value):
        value = jnp.transpose(value, (1, 0, 2, 3)).reshape(layers, fresh, KVH * HD)
        return jnp.pad(value, ((0, 0), (0, fresh_pad - fresh), (0, 0)))

    row = jnp.arange(requests * halves * rows)
    row_request = row // (halves * rows)
    row_step = row % rows // heads
    col = jnp.arange(fresh_pad)
    seen = (
        (col[None, :] % requests == row_request[:, None])
        & (col[None, :] // requests <= row_step[:, None])
        & (col[None, :] < fresh)
    )
    fresh_bias = jnp.where(seen, 0.0, NEG_BIG).astype(jnp.float32)
    quarter = n // 4
    block = cache.shape[1:]
    piece = (groups, layers, rows, HD)
    note = (groups, STAT_ROWS, HD)
    vmem = pl.BlockSpec(memory_space=pltpu.VMEM)
    smem = pl.BlockSpec(memory_space=pltpu.SMEM)
    dma = pltpu.SemaphoreType.DMA
    f32 = jnp.float32
    return pl.pallas_call(
        functools.partial(exchange_kernel, n, groups, halves),
        out_shape=(
            jax.ShapeDtypeStruct(cache.shape, cache.dtype),
            jax.ShapeDtypeStruct((steps, layers, share, HD), f32),
        ),
        in_specs=[smem] * 2 + [vmem] * 6,
        out_specs=(vmem, vmem),
        scratch_shapes=[
            pltpu.VMEM((n, cap) + block, cache.dtype),
            pltpu.VMEM((n, cap) + block, cache.dtype),
            pltpu.VMEM((2, 2, quarter) + piece, f32),
            pltpu.VMEM((2, quarter) + piece, f32),
            pltpu.VMEM((quarter,) + piece, f32),
            pltpu.VMEM((quarter,) + piece, f32),
            pltpu.VMEM((2, 2, quarter) + note, f32),
            pltpu.VMEM((2, quarter) + note, f32),
            pltpu.VMEM((quarter,) + note, f32),
            pltpu.VMEM((quarter,) + note, f32),
            pltpu.VMEM((requests * halves * rows, HD), f32),
            dma((n,)),
            dma((n,)),
            dma((4,)),
            dma((4,)),
            dma((2, quarter)),
            dma((2, quarter)),
        ],
        compiler_params=pltpu.CompilerParams(
            collective_id=0, has_side_effects=True, vmem_limit_bytes=56 * 1024 * 1024
        ),
        name="exchange",
    )(
        send_index,
        take_index,
        cache,
        q,
        fresh_rows(fresh_keys),
        fresh_rows(fresh_values),
        token_request,
        fresh_bias,
    )


def local(src_cache, src_blocks, dst_blocks, ctx_lengths, queries, new_keys, new_values):
    n = lax.axis_size("ctx")
    me = lax.axis_index("ctx")
    per_dev, _, _, block_len, _ = src_cache.shape
    total = src_blocks.shape[0]
    per_request = total // REQS
    cap = (per_dev + n - 1) // n
    slots = jnp.arange(total, dtype=jnp.int32)
    pos = jnp.arange(per_dev, dtype=jnp.int32)
    src_ids = lax.dynamic_slice_in_dim(src_blocks, me * per_dev, per_dev)
    dst_ids = lax.dynamic_slice_in_dim(dst_blocks, me * per_dev, per_dev)

    target = jnp.sum(jnp.where(src_ids[:, None] == dst_blocks[None], slots[None], 0), axis=1) // per_dev
    before = (target[:, None] == target[None]) & (pos[None] < pos[:, None])
    bucket = target * cap + jnp.sum(before.astype(jnp.int32), axis=1)
    bucket_ids = jnp.arange(n * cap, dtype=jnp.int32)
    chosen = jnp.sum(jnp.where(bucket_ids[:, None] == bucket[None], pos[None], 0), axis=1)

    root = jnp.sum(jnp.where(dst_ids[:, None] == src_blocks[None], slots[None], 0), axis=1)
    owner = root // per_dev
    earlier = (owner[:, None] == owner[None]) & (root[None] < root[:, None])
    rows = owner * cap + jnp.sum(earlier.astype(jnp.int32), axis=1)

    request = src_ids // per_request
    limit = jnp.sum(
        jnp.where(request[:, None] == jnp.arange(REQS)[None], ctx_lengths[None], 0), axis=1
    )
    at = (src_ids % per_request)[:, None] * block_len + jnp.arange(block_len)[None]
    token_request = jnp.where(at < limit[:, None], request[:, None], -1).astype(jnp.int32)
    token_request = token_request.reshape(1, per_dev * block_len)

    return exchange(
        n, cap, chosen, rows, src_cache, queries, new_keys, new_values, token_request
    )


def solution(mesh):
    in_specs = (
        P(("groups", "ctx"), None, None, None, None),
        P("groups"),
        P("groups"),
        P("groups"),
        P(None, None, "groups", None),
        P(None, None, "groups", None),
        P(None, None, "groups", None),
    )
    out_specs = (
        P(("groups", "ctx"), None, None, None, None),
        P(None, None, ("groups", "ctx"), None),
    )
    return jax.shard_map(local, mesh=mesh, in_specs=in_specs, out_specs=out_specs, check_vma=False)
```

```python
import functools

import jax
import jax.numpy as jnp
from jax import lax
from jax.experimental import pallas as pl
from jax.experimental.pallas import tpu as pltpu
from jax.sharding import PartitionSpec as P

KVH = 8
HD = 128
QPG = 16
REQS = 4

NEG_BIG = -1e30
STAT_ROWS = 8
MESH = pl.DeviceIdType.MESH


def plan_kernel(
    n, per_dev, block_len, per_request, src_ref, dst_ref, lengths, send_index, take_index, tokens_of
):
    me = lax.axis_index("ctx")
    cap = (per_dev + n - 1) // n
    total = src_ref.shape[1]
    f32 = jnp.float32

    def iota(cols, axis):
        return lax.broadcasted_iota(jnp.int32, (per_dev, cols), axis).astype(f32)

    def over(row, by):
        return jnp.floor(row * (1.0 / by))

    src, dst = src_ref[...].astype(f32), dst_ref[...].astype(f32)
    lane, sub = iota(total, 1), iota(total, 0)
    own = lane == sub + (me * per_dev).astype(f32)
    small_lane, small_sub = iota(per_dev, 1), iota(per_dev, 0)

    def column(mask, row):
        return jnp.sum(jnp.where(mask, row, 0.0), axis=1, keepdims=True)

    def as_row(col):
        return jnp.sum(jnp.where(small_lane == small_sub, col, 0.0), axis=0, keepdims=True)

    src_ids = column(own, src)
    dst_ids = column(own, dst)
    target = over(column(src_ids == dst, lane), per_dev)
    same = (target == as_row(target)) & (small_lane < small_sub)
    bucket = target * cap + column(same, 1.0)
    slots = iota(send_index.shape[1], 1)
    filled = jnp.where(bucket == slots, iota(send_index.shape[1], 0), 0.0)
    send_index[...] = jnp.sum(filled, axis=0, keepdims=True).astype(jnp.int32)

    root = column(dst_ids == src, lane)
    owner = over(root, per_dev)
    earlier = (owner == as_row(owner)) & (as_row(root) < root)
    take_index[...] = as_row(owner * cap + column(earlier, 1.0)).astype(jnp.int32)

    token, block = iota(per_dev * block_len, 1), iota(per_dev * block_len, 0)
    holds = over(token, block_len) == block
    ids = jnp.sum(jnp.where(holds, src_ids, 0.0), axis=0, keepdims=True)
    inner = token[:1] - over(token[:1], block_len) * block_len
    request = over(ids, per_request)
    at = (ids - request * per_request) * block_len + inner
    limit = jnp.zeros_like(at)
    for r in range(REQS):
        limit = jnp.where(request == r, lengths[r].astype(f32), limit)
    tokens_of[...] = jnp.where(at < limit, request, -1.0).astype(jnp.int32)


def plan(n, per_dev, block_len, src_blocks, dst_blocks, lengths):
    total = src_blocks.shape[0]
    slots = -(-n * ((per_dev + n - 1) // n) // HD) * HD
    vmem = pl.BlockSpec(memory_space=pltpu.VMEM)
    return pl.pallas_call(
        functools.partial(plan_kernel, n, per_dev, block_len, total // REQS),
        out_shape=(
            jax.ShapeDtypeStruct((1, slots), jnp.int32),
            jax.ShapeDtypeStruct((1, per_dev), jnp.int32),
            jax.ShapeDtypeStruct((1, per_dev * block_len), jnp.int32),
        ),
        in_specs=[vmem, vmem, pl.BlockSpec(memory_space=pltpu.SMEM)],
        out_specs=(vmem, vmem, vmem),
        name="plan",
    )(src_blocks.reshape(1, total), dst_blocks.reshape(1, total), lengths)


def place_kernel(index, arrived, placed, held, in_sems, out_sems):
    cap = arrived.shape[1]

    def read(i):
        at = index[0, i]
        return pltpu.make_async_copy(
            arrived.at[at // cap, lax.rem(at, cap)], held.at[i], in_sems.at[i]
        )

    def write(i):
        return pltpu.make_async_copy(held.at[i], placed.at[i], out_sems.at[i])

    def loop(body):
        lax.fori_loop(0, held.shape[0], lambda i, c: (body(i), c)[1], 0)

    loop(lambda i: read(i).start())
    loop(lambda i: (read(i).wait(), write(i).start()))
    loop(lambda i: write(i).wait())


def place(arrived, index):
    count = index.shape[1]
    shape = (count,) + arrived.shape[2:]
    dma = pltpu.SemaphoreType.DMA
    return pl.pallas_call(
        place_kernel,
        out_shape=jax.ShapeDtypeStruct(shape, arrived.dtype),
        in_specs=[pl.BlockSpec(memory_space=pltpu.SMEM), pl.BlockSpec(memory_space=pl.ANY)],
        out_specs=pl.BlockSpec(memory_space=pl.ANY),
        scratch_shapes=[pltpu.VMEM(shape, arrived.dtype), dma((count,)), dma((count,))],
        compiler_params=pltpu.CompilerParams(vmem_limit_bytes=16 * 1024 * 1024),
        name="place",
    )(index, arrived)


def split_bf16(value):
    high = value.astype(jnp.bfloat16)
    low = (value - high.astype(jnp.float32)).astype(jnp.bfloat16)
    return high, low


def dot(a, b, b_dim):
    return lax.dot_general(
        a, b, (((1,), (b_dim,)), ((), ())), preferred_element_type=jnp.float32
    )


def exchange_kernel(
    n,
    groups,
    halves,
    send_index,
    cache,
    queries,
    fresh_keys,
    fresh_values,
    token_request,
    arrived,
    result,
    outgoing,
    fresh_rows,
    fresh_bias,
    acc,
    acc_core,
    acc_near,
    acc_far,
    stat,
    stat_core,
    stat_near,
    stat_far,
    stat_cols,
    block_send,
    block_recv,
    pair_send,
    pair_recv,
    far_send,
    far_recv,
    own_sem,
):
    me = lax.axis_index("ctx")
    blocks, layers, _, block_len, _ = cache.shape
    tokens = blocks * block_len
    cap = outgoing.shape[1]
    quarter = n // 4
    rows = acc.shape[5]
    width = rows * halves
    bit0 = lax.rem(me, 2)
    bit1 = lax.rem(me // 2, 2)
    high = me // 4

    def loop(start, stop, body):
        lax.fori_loop(start, stop, lambda k, c: (body(k), c)[1], 0)

    def peer(k):
        return lax.rem(me + k, n)

    def send(src, dst, send_sem, recv_sem, device):
        return pltpu.make_async_remote_copy(
            src_ref=src,
            dst_ref=dst,
            send_sem=send_sem,
            recv_sem=recv_sem,
            device_id={"ctx": device},
            device_id_type=MESH,
        )

    barrier = pltpu.get_barrier_semaphore()
    loop(
        1,
        n,
        lambda k: pl.semaphore_signal(
            barrier, 1, device_id={"ctx": peer(k)}, device_id_type=MESH
        ),
    )
    pl.semaphore_wait(barrier, n - 1)

    def block_copy(k):
        return send(
            outgoing.at[peer(k)], arrived.at[me], block_send.at[k], block_recv.at[k], peer(k)
        )

    def fill(to):
        for c in range(cap):
            outgoing[to, c] = cache[send_index[0, to * cap + c]]

    def shift(i):
        j = i // 2
        odd = lax.rem(j, 2)
        far = n // 2 + odd * (j + 1) // 2 - (1 - odd) * (j // 2)
        near = (1 - odd) * (1 + j // 2) + odd * (n - (j + 1) // 2)
        pick = lax.rem(i, 2)
        return (1 - pick) * far + pick * near

    def send_blocks(i):
        k = shift(i)
        fill(peer(k))
        block_copy(k).start()

    windows = [0, n * 5 // 16, n * 7 // 16, n * 10 // 16, n - 1]

    def send_window(w):
        loop(windows[w], windows[w + 1], send_blocks)

    send_window(0)
    fill(me)
    own_copy = pltpu.make_async_copy(outgoing.at[me], arrived.at[me], own_sem.at[0])
    own_copy.start()

    steps = queries.shape[0]
    heads = rows // steps
    fresh = steps * REQS
    for which, value in ((0, fresh_keys), (1, fresh_values)):
        for layer in range(layers):
            parts = [value[u, layer].astype(jnp.float32) for u in range(steps)]
            parts.append(jnp.zeros((fresh_rows.shape[2] - fresh, KVH * HD), jnp.float32))
            fresh_rows[which, layer] = jnp.concatenate(parts, axis=0).astype(jnp.bfloat16)
    bias_shape = (width, fresh_rows.shape[2])
    row = lax.broadcasted_iota(jnp.int32, bias_shape, 0)
    col = lax.broadcasted_iota(jnp.int32, bias_shape, 1)
    for h in range(1, halves):
        row = jnp.where(row >= rows, row - rows, row)
    row_step = sum((row >= heads * j).astype(jnp.int32) for j in range(1, steps))
    col_step = sum((col >= REQS * j).astype(jnp.int32) for j in range(1, steps))
    col_request = col - REQS * col_step
    usable = (col_step <= row_step) & (col < fresh) & (me == 0)
    for r in range(REQS):
        fresh_bias[r * width : (r + 1) * width] = jnp.where(
            usable & (col_request == r), 0.0, NEG_BIG
        )

    stat_cols[...] = jnp.zeros_like(stat_cols)
    lane = lax.broadcasted_iota(jnp.int32, (1, HD), 1)

    def query_rows(layer, g):
        span = pl.ds(pl.multiple_of(g * QPG * HD, QPG * HD), QPG * HD)
        parts = [
            queries[step, layer, :, span].astype(jnp.float32).reshape(REQS, QPG, HD)
            for step in range(steps)
        ]
        ordered = [
            parts[step][r, h * heads : (h + 1) * heads]
            for r in range(REQS)
            for h in range(halves)
            for step in range(steps)
        ]
        return jnp.concatenate(ordered, axis=0).astype(jnp.bfloat16)

    def head(g):
        cols = pl.ds(pl.multiple_of(g * HD, HD), HD)
        for layer in range(layers):
            q = query_rows(layer, g)
            k_cache = cache[:, layer, 0, :, cols].reshape(tokens, HD)
            v_cache = cache[:, layer, 1, :, cols].reshape(tokens, HD)
            k_new = fresh_rows[0, layer, :, cols]
            v_new = fresh_rows[1, layer, :, cols]
            scores = dot(q, k_cache, 1) * (HD**-0.5)
            new_scores = dot(q, k_new, 1) * (HD**-0.5)
            for r in range(REQS):
                part = slice(r * width, (r + 1) * width)
                live = jnp.where(token_request[...] == r, 0.0, NEG_BIG)
                s = scores[part] + live
                s_new = new_scores[part] + fresh_bias[part]
                top = jnp.maximum(
                    jnp.max(s, axis=1, keepdims=True), jnp.max(s_new, axis=1, keepdims=True)
                )
                w = jnp.exp(s - top)
                w_new = jnp.exp(s_new - top)
                total = jnp.sum(w, axis=1, keepdims=True) + jnp.sum(w_new, axis=1, keepdims=True)
                big, small = split_bf16(w)
                new_big, new_small = split_bf16(w_new)
                sums = (
                    dot(big, v_cache, 0)
                    + dot(small, v_cache, 0)
                    + dot(new_big, v_new, 0)
                    + dot(new_small, v_new, 0)
                )
                for h in range(halves):
                    chunk = (r * KVH + g) * halves + h
                    to, gi = chunk // groups, chunk % groups
                    acc[to % 2, to // 2 % 2, to // 4, gi, layer] = sums[h * rows : (h + 1) * rows]
                at = g * STAT_ROWS + layer
                now = stat_cols[part]
                now = jnp.where(lane == at, top, now)
                stat_cols[part] = jnp.where(lane == at + layers, total, now)

    loop(0, KVH, head)

    pad = jnp.zeros((HD - rows, HD), jnp.float32)
    for r in range(REQS):
        for h in range(halves):
            start = (r * halves + h) * rows
            turned = jnp.concatenate([stat_cols[start : start + rows], pad], axis=0).T
            for g in range(KVH):
                chunk = (r * KVH + g) * halves + h
                to, gi = chunk // groups, chunk % groups
                stat[to % 2, to // 2 % 2, to // 4, gi] = turned[
                    g * STAT_ROWS : (g + 1) * STAT_ROWS
                ]

    def columns(factors):
        filler = jnp.zeros((HD - factors.shape[0], HD), jnp.float32)
        return jnp.concatenate([factors, filler], axis=0).T

    def join(acc_own, stat_own, acc_new, stat_new):
        for gi in range(groups):
            a, b = stat_own[gi], stat_new[gi]
            top = jnp.maximum(a[:layers], b[:layers])
            keep = jnp.exp(a[:layers] - top)
            add = jnp.exp(b[:layers] - top)
            total = a[layers : 2 * layers] * keep + b[layers : 2 * layers] * add
            filler = jnp.zeros((STAT_ROWS - 2 * layers, HD), jnp.float32)
            stat_own[gi] = jnp.concatenate([top, total, filler], axis=0)
            factor = columns(jnp.concatenate([keep, add], axis=0))
            for layer in range(layers):
                acc_own[gi, layer] = (
                    acc_own[gi, layer] * factor[:rows, layer : layer + 1]
                    + acc_new[gi, layer] * factor[:rows, layers + layer : layers + layer + 1]
                )

    def swap(copies, window):
        for copy in copies:
            copy.start()
        send_window(window)
        for copy in copies:
            copy.wait()

    core = me + 1 - 2 * bit0
    swap(
        [
            send(stat.at[1 - bit0], stat_core, pair_send.at[0], pair_recv.at[0], core),
            send(acc.at[1 - bit0], acc_core, pair_send.at[1], pair_recv.at[1], core),
        ],
        1,
    )

    def join_core(i):
        b, z = i // quarter, lax.rem(i, quarter)
        join(
            acc.at[bit0, b, z], stat.at[bit0, b, z], acc_core.at[b, z], stat_core.at[b, z]
        )

    loop(0, 2 * quarter, join_core)

    near = me + 2 - 4 * bit1
    swap(
        [
            send(stat.at[bit0, 1 - bit1], stat_near, pair_send.at[2], pair_recv.at[2], near),
            send(acc.at[bit0, 1 - bit1], acc_near, pair_send.at[3], pair_recv.at[3], near),
        ],
        2,
    )
    loop(
        0,
        quarter,
        lambda z: join(
            acc.at[bit0, bit1, z], stat.at[bit0, bit1, z], acc_near.at[z], stat_near.at[z]
        ),
    )

    def far_copies(k):
        to = lax.rem(high + k, quarter)
        device = to * 4 + lax.rem(me, 4)
        return (
            send(
                stat.at[bit0, bit1, to],
                stat_far.at[high],
                far_send.at[0, k],
                far_recv.at[0, k],
                device,
            ),
            send(
                acc.at[bit0, bit1, to], acc_far.at[high], far_send.at[1, k], far_recv.at[1, k], device
            ),
        )

    loop(1, quarter, lambda k: [copy.start() for copy in far_copies(k)])
    send_window(3)
    stat_far[high] = stat[bit0, bit1, high]
    acc_far[high] = acc[bit0, bit1, high]
    loop(1, quarter, lambda k: [copy.wait() for copy in far_copies(k)])

    share = rows // result.shape[0]
    for gi in range(groups):
        for layer in range(layers):
            tops = stat_far[:, gi, layer, :]
            top = jnp.max(tops, axis=0, keepdims=True)
            factor = jnp.exp(tops - top)
            total = jnp.sum(factor * stat_far[:, gi, layers + layer, :], axis=0, keepdims=True)
            factor = columns(factor / total)
            out = jnp.zeros((rows, HD), jnp.float32)
            for src in range(quarter):
                out = out + factor[:rows, src : src + 1] * acc_far[src, gi, layer]
            for step in range(result.shape[0]):
                result[step, layer, gi * share : (gi + 1) * share, :] = out[
                    step * share : (step + 1) * share
                ]

    own_copy.wait()
    loop(1, n, lambda k: block_copy(k).wait())


def exchange(n, cap, send_index, cache, queries, fresh_keys, fresh_values, token_request):
    steps, layers, requests, _ = queries.shape
    share = requests * KVH * QPG // n
    groups = max(share // QPG, 1)
    halves = max(QPG // share, 1)
    heads = QPG // halves
    rows = steps * heads
    fresh_pad = -(-steps * requests // 16) * 16
    quarter = n // 4
    block = cache.shape[1:]
    piece = (groups, layers, rows, HD)
    note = (groups, STAT_ROWS, HD)
    vmem = pl.BlockSpec(memory_space=pltpu.VMEM)
    smem = pl.BlockSpec(memory_space=pltpu.SMEM)
    dma = pltpu.SemaphoreType.DMA
    f32 = jnp.float32
    return pl.pallas_call(
        functools.partial(exchange_kernel, n, groups, halves),
        out_shape=(
            jax.ShapeDtypeStruct((n, cap) + block, cache.dtype),
            jax.ShapeDtypeStruct((steps, layers, share, HD), f32),
        ),
        in_specs=[smem] + [vmem] * 5,
        out_specs=(pl.BlockSpec(memory_space=pl.ANY), vmem),
        scratch_shapes=[
            pltpu.VMEM((n, cap) + block, cache.dtype),
            pltpu.VMEM((2, layers, fresh_pad, KVH * HD), cache.dtype),
            pltpu.VMEM((requests * halves * rows, fresh_pad), f32),
            pltpu.VMEM((2, 2, quarter) + piece, f32),
            pltpu.VMEM((2, quarter) + piece, f32),
            pltpu.VMEM((quarter,) + piece, f32),
            pltpu.VMEM((quarter,) + piece, f32),
            pltpu.VMEM((2, 2, quarter) + note, f32),
            pltpu.VMEM((2, quarter) + note, f32),
            pltpu.VMEM((quarter,) + note, f32),
            pltpu.VMEM((quarter,) + note, f32),
            pltpu.VMEM((requests * halves * rows, HD), f32),
            dma((n,)),
            dma((n,)),
            dma((4,)),
            dma((4,)),
            dma((2, quarter)),
            dma((2, quarter)),
            dma((1,)),
        ],
        compiler_params=pltpu.CompilerParams(
            collective_id=0, has_side_effects=True, vmem_limit_bytes=56 * 1024 * 1024
        ),
        name="exchange",
    )(send_index, cache, queries, fresh_keys, fresh_values, token_request)


def local(src_cache, src_blocks, dst_blocks, ctx_lengths, queries, new_keys, new_values):
    n = lax.axis_size("ctx")
    per_dev, _, _, block_len, _ = src_cache.shape
    cap = (per_dev + n - 1) // n
    send_index, take_index, token_request = plan(
        n, per_dev, block_len, src_blocks, dst_blocks, ctx_lengths
    )
    arrived, attn = exchange(
        n, cap, send_index, src_cache, queries, new_keys, new_values, token_request
    )
    return place(arrived, take_index), attn


def solution(mesh):
    in_specs = (
        P(("groups", "ctx"), None, None, None, None),
        P("groups"),
        P("groups"),
        P("groups"),
        P(None, None, "groups", None),
        P(None, None, "groups", None),
        P(None, None, "groups", None),
    )
    out_specs = (
        P(("groups", "ctx"), None, None, None, None),
        P(None, None, ("groups", "ctx"), None),
    )
    return jax.shard_map(local, mesh=mesh, in_specs=in_specs, out_specs=out_specs, check_vma=False)
```

```python
import functools

import jax
import jax.numpy as jnp
from jax import lax
from jax.experimental import pallas as pl
from jax.experimental.pallas import tpu as pltpu
from jax.sharding import PartitionSpec as P

KVH = 8
HD = 128
QPG = 16
REQS = 4

NEG_BIG = -1e30
STAT_ROWS = 8
MESH = pl.DeviceIdType.MESH


def plan_kernel(
    n, per_dev, block_len, per_request, src_ref, dst_ref, lengths, send_index, take_index, tokens_of
):
    me = lax.axis_index("ctx")
    cap = (per_dev + n - 1) // n
    total = src_ref.shape[1]
    f32 = jnp.float32

    def iota(cols, axis):
        return lax.broadcasted_iota(jnp.int32, (per_dev, cols), axis).astype(f32)

    def over(row, by):
        return jnp.floor(row * (1.0 / by))

    src, dst = src_ref[...].astype(f32), dst_ref[...].astype(f32)
    lane, sub = iota(total, 1), iota(total, 0)
    own = lane == sub + (me * per_dev).astype(f32)
    small_lane, small_sub = iota(per_dev, 1), iota(per_dev, 0)

    def column(mask, row):
        return jnp.sum(jnp.where(mask, row, 0.0), axis=1, keepdims=True)

    def as_row(col):
        return jnp.sum(jnp.where(small_lane == small_sub, col, 0.0), axis=0, keepdims=True)

    src_ids = column(own, src)
    dst_ids = column(own, dst)
    target = over(column(src_ids == dst, lane), per_dev)
    same = (target == as_row(target)) & (small_lane < small_sub)
    bucket = target * cap + column(same, 1.0)
    slots = iota(send_index.shape[1], 1)
    filled = jnp.where(bucket == slots, iota(send_index.shape[1], 0), 0.0)
    send_index[...] = jnp.sum(filled, axis=0, keepdims=True).astype(jnp.int32)

    root = column(dst_ids == src, lane)
    owner = over(root, per_dev)
    earlier = (owner == as_row(owner)) & (as_row(root) < root)
    take_index[...] = as_row(owner * cap + column(earlier, 1.0)).astype(jnp.int32)

    token, block = iota(per_dev * block_len, 1), iota(per_dev * block_len, 0)
    holds = over(token, block_len) == block
    ids = jnp.sum(jnp.where(holds, src_ids, 0.0), axis=0, keepdims=True)
    inner = token[:1] - over(token[:1], block_len) * block_len
    request = over(ids, per_request)
    at = (ids - request * per_request) * block_len + inner
    limit = jnp.zeros_like(at)
    for r in range(REQS):
        limit = jnp.where(request == r, lengths[r].astype(f32), limit)
    tokens_of[...] = jnp.where(at < limit, request, -1.0).astype(jnp.int32)


def plan(n, per_dev, block_len, src_blocks, dst_blocks, lengths):
    total = src_blocks.shape[0]
    slots = -(-n * ((per_dev + n - 1) // n) // HD) * HD
    vmem = pl.BlockSpec(memory_space=pltpu.VMEM)
    return pl.pallas_call(
        functools.partial(plan_kernel, n, per_dev, block_len, total // REQS),
        out_shape=(
            jax.ShapeDtypeStruct((1, slots), jnp.int32),
            jax.ShapeDtypeStruct((1, per_dev), jnp.int32),
            jax.ShapeDtypeStruct((1, per_dev * block_len), jnp.int32),
        ),
        in_specs=[vmem, vmem, pl.BlockSpec(memory_space=pltpu.SMEM)],
        out_specs=(vmem, vmem, vmem),
        name="plan",
    )(src_blocks.reshape(1, total), dst_blocks.reshape(1, total), lengths)


def place_kernel(
    index, arrived, attn, placed, result, held, held_attn, in_sems, out_sems, attn_sems
):
    cap = arrived.shape[1]

    def read(i):
        at = index[0, i]
        return pltpu.make_async_copy(
            arrived.at[at // cap, lax.rem(at, cap)], held.at[i], in_sems.at[i]
        )

    def write(i):
        return pltpu.make_async_copy(held.at[i], placed.at[i], out_sems.at[i])

    def loop(body):
        lax.fori_loop(0, held.shape[0], lambda i, c: (body(i), c)[1], 0)

    attn_in = pltpu.make_async_copy(attn, held_attn, attn_sems.at[0])
    attn_out = pltpu.make_async_copy(held_attn, result, attn_sems.at[1])
    attn_in.start()
    loop(lambda i: read(i).start())
    attn_in.wait()
    attn_out.start()
    loop(lambda i: (read(i).wait(), write(i).start()))
    loop(lambda i: write(i).wait())
    attn_out.wait()


def place(arrived, attn, index):
    count = index.shape[1]
    shape = (count,) + arrived.shape[2:]
    dma = pltpu.SemaphoreType.DMA
    hbm = pl.BlockSpec(memory_space=pl.ANY)
    return pl.pallas_call(
        place_kernel,
        out_shape=(
            jax.ShapeDtypeStruct(shape, arrived.dtype),
            jax.ShapeDtypeStruct(attn.shape, attn.dtype),
        ),
        in_specs=[pl.BlockSpec(memory_space=pltpu.SMEM), hbm, hbm],
        out_specs=(hbm, hbm),
        scratch_shapes=[
            pltpu.VMEM(shape, arrived.dtype),
            pltpu.VMEM(attn.shape, attn.dtype),
            dma((count,)),
            dma((count,)),
            dma((2,)),
        ],
        compiler_params=pltpu.CompilerParams(vmem_limit_bytes=60 * 1024 * 1024),
        name="place",
    )(index, arrived, attn)


def split_bf16(value):
    high = value.astype(jnp.bfloat16)
    low = (value - high.astype(jnp.float32)).astype(jnp.bfloat16)
    return high, low


def dot(a, b, b_dim):
    return lax.dot_general(
        a, b, (((1,), (b_dim,)), ((), ())), preferred_element_type=jnp.float32
    )


def exchange_kernel(
    n,
    groups,
    halves,
    send_index,
    cache_ref,
    queries_ref,
    fresh_keys,
    fresh_values,
    token_request,
    arrived,
    result,
    cache,
    queries,
    outgoing,
    fresh_rows,
    fresh_bias,
    acc,
    acc_core,
    acc_near,
    acc_far,
    stat,
    stat_core,
    stat_near,
    stat_far,
    stat_cols,
    block_send,
    block_recv,
    pair_send,
    pair_recv,
    far_send,
    far_recv,
    own_sem,
):
    me = lax.axis_index("ctx")
    blocks, layers, _, block_len, _ = cache.shape
    tokens = blocks * block_len
    cap = outgoing.shape[1]
    quarter = n // 4
    rows = acc.shape[5]
    width = rows * halves
    bit0 = lax.rem(me, 2)
    bit1 = lax.rem(me // 2, 2)
    high = me // 4

    def loop(start, stop, body):
        lax.fori_loop(start, stop, lambda k, c: (body(k), c)[1], 0)

    def peer(k):
        return lax.rem(me + k, n)

    def send(src, dst, send_sem, recv_sem, device):
        return pltpu.make_async_remote_copy(
            src_ref=src,
            dst_ref=dst,
            send_sem=send_sem,
            recv_sem=recv_sem,
            device_id={"ctx": device},
            device_id_type=MESH,
        )

    cache_load = pltpu.make_async_copy(cache_ref, cache, own_sem.at[1])
    queries_load = pltpu.make_async_copy(queries_ref, queries, own_sem.at[2])
    cache_load.start()
    queries_load.start()

    barrier = pltpu.get_barrier_semaphore()
    loop(
        1,
        n,
        lambda k: pl.semaphore_signal(
            barrier, 1, device_id={"ctx": peer(k)}, device_id_type=MESH
        ),
    )
    pl.semaphore_wait(barrier, n - 1)
    cache_load.wait()

    def block_copy(k):
        return send(
            outgoing.at[peer(k)], arrived.at[me], block_send.at[k], block_recv.at[k], peer(k)
        )

    def fill(to):
        for c in range(cap):
            outgoing[to, c] = cache[send_index[0, to * cap + c]]

    def shift(i):
        j = i // 2
        odd = lax.rem(j, 2)
        far = n // 2 + odd * (j + 1) // 2 - (1 - odd) * (j // 2)
        near = (1 - odd) * (1 + j // 2) + odd * (n - (j + 1) // 2)
        pick = lax.rem(i, 2)
        return (1 - pick) * far + pick * near

    def send_blocks(i):
        k = shift(i)
        fill(peer(k))
        block_copy(k).start()

    windows = [0, n // 4, n // 2, n * 5 // 8, n * 3 // 4, n - 1]

    def send_window(w):
        loop(windows[w], windows[w + 1], send_blocks)

    send_window(0)
    fill(me)
    own_copy = pltpu.make_async_copy(outgoing.at[me], arrived.at[me], own_sem.at[0])
    own_copy.start()

    steps = queries.shape[0]
    heads = rows // steps
    fresh = steps * REQS
    for which, value in ((0, fresh_keys), (1, fresh_values)):
        for layer in range(layers):
            parts = [value[u, layer].astype(jnp.float32) for u in range(steps)]
            parts.append(jnp.zeros((fresh_rows.shape[2] - fresh, KVH * HD), jnp.float32))
            fresh_rows[which, layer] = jnp.concatenate(parts, axis=0).astype(jnp.bfloat16)
    bias_shape = (width, fresh_rows.shape[2])
    row = lax.broadcasted_iota(jnp.int32, bias_shape, 0)
    col = lax.broadcasted_iota(jnp.int32, bias_shape, 1)
    for h in range(1, halves):
        row = jnp.where(row >= rows, row - rows, row)
    row_step = sum((row >= heads * j).astype(jnp.int32) for j in range(1, steps))
    col_step = sum((col >= REQS * j).astype(jnp.int32) for j in range(1, steps))
    col_request = col - REQS * col_step
    usable = (col_step <= row_step) & (col < fresh) & (me == 0)
    for r in range(REQS):
        fresh_bias[r * width : (r + 1) * width] = jnp.where(
            usable & (col_request == r), 0.0, NEG_BIG
        )

    stat_cols[...] = jnp.zeros_like(stat_cols)
    lane = lax.broadcasted_iota(jnp.int32, (1, HD), 1)

    def query_rows(layer, g):
        span = pl.ds(pl.multiple_of(g * QPG * HD, QPG * HD), QPG * HD)
        parts = [
            queries[step, layer, :, span].astype(jnp.float32).reshape(REQS, QPG, HD)
            for step in range(steps)
        ]
        ordered = [
            parts[step][r, h * heads : (h + 1) * heads]
            for r in range(REQS)
            for h in range(halves)
            for step in range(steps)
        ]
        return jnp.concatenate(ordered, axis=0).astype(jnp.bfloat16)

    def head(g):
        cols = pl.ds(pl.multiple_of(g * HD, HD), HD)
        for layer in range(layers):
            q = query_rows(layer, g)
            k_cache = cache[:, layer, 0, :, cols].reshape(tokens, HD)
            v_cache = cache[:, layer, 1, :, cols].reshape(tokens, HD)
            k_new = fresh_rows[0, layer, :, cols]
            v_new = fresh_rows[1, layer, :, cols]
            scores = dot(q, k_cache, 1) * (HD**-0.5)
            new_scores = dot(q, k_new, 1) * (HD**-0.5)
            for r in range(REQS):
                part = slice(r * width, (r + 1) * width)
                live = jnp.where(token_request[...] == r, 0.0, NEG_BIG)
                s = scores[part] + live
                s_new = new_scores[part] + fresh_bias[part]
                top = jnp.maximum(
                    jnp.max(s, axis=1, keepdims=True), jnp.max(s_new, axis=1, keepdims=True)
                )
                w = jnp.exp(s - top)
                w_new = jnp.exp(s_new - top)
                total = jnp.sum(w, axis=1, keepdims=True) + jnp.sum(w_new, axis=1, keepdims=True)
                big, small = split_bf16(w)
                new_big, new_small = split_bf16(w_new)
                sums = (
                    dot(big, v_cache, 0)
                    + dot(small, v_cache, 0)
                    + dot(new_big, v_new, 0)
                    + dot(new_small, v_new, 0)
                )
                for h in range(halves):
                    chunk = (r * KVH + g) * halves + h
                    to, gi = chunk // groups, chunk % groups
                    acc[to % 2, to // 2 % 2, to // 4, gi, layer] = sums[h * rows : (h + 1) * rows]
                at = g * STAT_ROWS + layer
                now = stat_cols[part]
                now = jnp.where(lane == at, top, now)
                stat_cols[part] = jnp.where(lane == at + layers, total, now)

    queries_load.wait()
    span = windows[2] - windows[1]
    stops = KVH // 2

    def head_pair(i):
        loop(2 * i, 2 * i + 2, head)
        loop(
            windows[1] + lax.div(span * i, stops),
            windows[1] + lax.div(span * (i + 1), stops),
            send_blocks,
        )

    loop(0, stops, head_pair)

    pad = jnp.zeros((HD - rows, HD), jnp.float32)
    for r in range(REQS):
        for h in range(halves):
            start = (r * halves + h) * rows
            turned = jnp.concatenate([stat_cols[start : start + rows], pad], axis=0).T
            for g in range(KVH):
                chunk = (r * KVH + g) * halves + h
                to, gi = chunk // groups, chunk % groups
                stat[to % 2, to // 2 % 2, to // 4, gi] = turned[
                    g * STAT_ROWS : (g + 1) * STAT_ROWS
                ]

    def columns(factors):
        filler = jnp.zeros((HD - factors.shape[0], HD), jnp.float32)
        return jnp.concatenate([factors, filler], axis=0).T

    def join(acc_own, stat_own, acc_new, stat_new):
        for gi in range(groups):
            a, b = stat_own[gi], stat_new[gi]
            top = jnp.maximum(a[:layers], b[:layers])
            keep = jnp.exp(a[:layers] - top)
            add = jnp.exp(b[:layers] - top)
            total = a[layers : 2 * layers] * keep + b[layers : 2 * layers] * add
            filler = jnp.zeros((STAT_ROWS - 2 * layers, HD), jnp.float32)
            stat_own[gi] = jnp.concatenate([top, total, filler], axis=0)
            factor = columns(jnp.concatenate([keep, add], axis=0))
            for layer in range(layers):
                acc_own[gi, layer] = (
                    acc_own[gi, layer] * factor[:rows, layer : layer + 1]
                    + acc_new[gi, layer] * factor[:rows, layers + layer : layers + layer + 1]
                )

    def swap(copies, window):
        for copy in copies:
            copy.start()
        send_window(window)
        for copy in copies:
            copy.wait()

    core = me + 1 - 2 * bit0
    swap(
        [
            send(stat.at[1 - bit0], stat_core, pair_send.at[0], pair_recv.at[0], core),
            send(acc.at[1 - bit0], acc_core, pair_send.at[1], pair_recv.at[1], core),
        ],
        2,
    )

    def join_core(i):
        b, z = i // quarter, lax.rem(i, quarter)
        join(
            acc.at[bit0, b, z], stat.at[bit0, b, z], acc_core.at[b, z], stat_core.at[b, z]
        )

    loop(0, 2 * quarter, join_core)

    near = me + 2 - 4 * bit1
    swap(
        [
            send(stat.at[bit0, 1 - bit1], stat_near, pair_send.at[2], pair_recv.at[2], near),
            send(acc.at[bit0, 1 - bit1], acc_near, pair_send.at[3], pair_recv.at[3], near),
        ],
        3,
    )
    loop(
        0,
        quarter,
        lambda z: join(
            acc.at[bit0, bit1, z], stat.at[bit0, bit1, z], acc_near.at[z], stat_near.at[z]
        ),
    )

    def far_copies(k):
        to = lax.rem(high + k, quarter)
        device = to * 4 + lax.rem(me, 4)
        return (
            send(
                stat.at[bit0, bit1, to],
                stat_far.at[high],
                far_send.at[0, k],
                far_recv.at[0, k],
                device,
            ),
            send(
                acc.at[bit0, bit1, to], acc_far.at[high], far_send.at[1, k], far_recv.at[1, k], device
            ),
        )

    loop(1, quarter, lambda k: [copy.start() for copy in far_copies(k)])
    send_window(4)
    stat_far[high] = stat[bit0, bit1, high]
    acc_far[high] = acc[bit0, bit1, high]
    loop(1, quarter, lambda k: [copy.wait() for copy in far_copies(k)])

    share = rows // result.shape[0]
    for gi in range(groups):
        for layer in range(layers):
            tops = stat_far[:, gi, layer, :]
            top = jnp.max(tops, axis=0, keepdims=True)
            factor = jnp.exp(tops - top)
            total = jnp.sum(factor * stat_far[:, gi, layers + layer, :], axis=0, keepdims=True)
            factor = columns(factor / total)
            out = jnp.zeros((rows, HD), jnp.float32)
            for src in range(quarter):
                out = out + factor[:rows, src : src + 1] * acc_far[src, gi, layer]
            for step in range(result.shape[0]):
                result[step, layer, gi * share : (gi + 1) * share, :] = out[
                    step * share : (step + 1) * share
                ]

    own_copy.wait()
    loop(1, n, lambda k: block_copy(k).wait())


def exchange(n, cap, send_index, cache, queries, fresh_keys, fresh_values, token_request):
    steps, layers, requests, _ = queries.shape
    share = requests * KVH * QPG // n
    groups = max(share // QPG, 1)
    halves = max(QPG // share, 1)
    heads = QPG // halves
    rows = steps * heads
    fresh_pad = -(-steps * requests // 16) * 16
    quarter = n // 4
    block = cache.shape[1:]
    piece = (groups, layers, rows, HD)
    note = (groups, STAT_ROWS, HD)
    vmem = pl.BlockSpec(memory_space=pltpu.VMEM)
    smem = pl.BlockSpec(memory_space=pltpu.SMEM)
    hbm = pl.BlockSpec(memory_space=pl.ANY)
    dma = pltpu.SemaphoreType.DMA
    f32 = jnp.float32
    return pl.pallas_call(
        functools.partial(exchange_kernel, n, groups, halves),
        out_shape=(
            jax.ShapeDtypeStruct((n, cap) + block, cache.dtype),
            jax.ShapeDtypeStruct((steps, layers, share, HD), f32),
        ),
        in_specs=[smem, hbm, hbm] + [vmem] * 3,
        out_specs=(hbm, vmem),
        scratch_shapes=[
            pltpu.VMEM(cache.shape, cache.dtype),
            pltpu.VMEM(queries.shape, queries.dtype),
            pltpu.VMEM((n, cap) + block, cache.dtype),
            pltpu.VMEM((2, layers, fresh_pad, KVH * HD), cache.dtype),
            pltpu.VMEM((requests * halves * rows, fresh_pad), f32),
            pltpu.VMEM((2, 2, quarter) + piece, f32),
            pltpu.VMEM((2, quarter) + piece, f32),
            pltpu.VMEM((quarter,) + piece, f32),
            pltpu.VMEM((quarter,) + piece, f32),
            pltpu.VMEM((2, 2, quarter) + note, f32),
            pltpu.VMEM((2, quarter) + note, f32),
            pltpu.VMEM((quarter,) + note, f32),
            pltpu.VMEM((quarter,) + note, f32),
            pltpu.VMEM((requests * halves * rows, HD), f32),
            dma((n,)),
            dma((n,)),
            dma((4,)),
            dma((4,)),
            dma((2, quarter)),
            dma((2, quarter)),
            dma((3,)),
        ],
        compiler_params=pltpu.CompilerParams(
            collective_id=0, has_side_effects=True, vmem_limit_bytes=56 * 1024 * 1024
        ),
        name="exchange",
    )(send_index, cache, queries, fresh_keys, fresh_values, token_request)


def local(src_cache, src_blocks, dst_blocks, ctx_lengths, queries, new_keys, new_values):
    n = lax.axis_size("ctx")
    per_dev, _, _, block_len, _ = src_cache.shape
    cap = (per_dev + n - 1) // n
    send_index, take_index, token_request = plan(
        n, per_dev, block_len, src_blocks, dst_blocks, ctx_lengths
    )
    arrived, attn = exchange(
        n, cap, send_index, src_cache, queries, new_keys, new_values, token_request
    )
    return place(arrived, attn, take_index)


def solution(mesh):
    in_specs = (
        P(("groups", "ctx"), None, None, None, None),
        P("groups"),
        P("groups"),
        P("groups"),
        P(None, None, "groups", None),
        P(None, None, "groups", None),
        P(None, None, "groups", None),
    )
    out_specs = (
        P(("groups", "ctx"), None, None, None, None),
        P(None, None, ("groups", "ctx"), None),
    )
    return jax.shard_map(local, mesh=mesh, in_specs=in_specs, out_specs=out_specs, check_vma=False)
```

```python
import functools

import jax
import jax.numpy as jnp
from jax import lax
from jax.experimental import pallas as pl
from jax.experimental.pallas import tpu as pltpu
from jax.sharding import PartitionSpec as P

KVH = 8
HD = 128
QPG = 16
REQS = 4

NEG_BIG = -1e30
STAT_ROWS = 8
MESH = pl.DeviceIdType.MESH


def plan_kernel(
    n, per_dev, block_len, per_request, src_ref, dst_ref, lengths, send_index, take_index, tokens_of
):
    me = lax.axis_index("ctx")
    cap = (per_dev + n - 1) // n
    total = src_ref.shape[1]
    f32 = jnp.float32

    def iota(cols, axis):
        return lax.broadcasted_iota(jnp.int32, (per_dev, cols), axis).astype(f32)

    def over(row, by):
        return jnp.floor(row * (1.0 / by))

    src, dst = src_ref[...].astype(f32), dst_ref[...].astype(f32)
    lane, sub = iota(total, 1), iota(total, 0)
    own = lane == sub + (me * per_dev).astype(f32)
    small_lane, small_sub = iota(per_dev, 1), iota(per_dev, 0)

    def column(mask, row):
        return jnp.sum(jnp.where(mask, row, 0.0), axis=1, keepdims=True)

    def as_row(col):
        return jnp.sum(jnp.where(small_lane == small_sub, col, 0.0), axis=0, keepdims=True)

    src_ids = column(own, src)
    dst_ids = column(own, dst)
    target = over(column(src_ids == dst, lane), per_dev)
    same = (target == as_row(target)) & (small_lane < small_sub)
    bucket = target * cap + column(same, 1.0)
    slots = iota(send_index.shape[1], 1)
    filled = jnp.where(bucket == slots, iota(send_index.shape[1], 0), 0.0)
    send_index[...] = jnp.sum(filled, axis=0, keepdims=True).astype(jnp.int32)

    root = column(dst_ids == src, lane)
    owner = over(root, per_dev)
    earlier = (owner == as_row(owner)) & (as_row(root) < root)
    take_index[...] = as_row(owner * cap + column(earlier, 1.0)).astype(jnp.int32)

    token, block = iota(per_dev * block_len, 1), iota(per_dev * block_len, 0)
    holds = over(token, block_len) == block
    ids = jnp.sum(jnp.where(holds, src_ids, 0.0), axis=0, keepdims=True)
    inner = token[:1] - over(token[:1], block_len) * block_len
    request = over(ids, per_request)
    at = (ids - request * per_request) * block_len + inner
    limit = jnp.zeros_like(at)
    for r in range(REQS):
        limit = jnp.where(request == r, lengths[r].astype(f32), limit)
    tokens_of[...] = jnp.where(at < limit, request, -1.0).astype(jnp.int32)


def plan(n, per_dev, block_len, src_blocks, dst_blocks, lengths):
    total = src_blocks.shape[0]
    slots = -(-n * ((per_dev + n - 1) // n) // HD) * HD
    vmem = pl.BlockSpec(memory_space=pltpu.VMEM)
    return pl.pallas_call(
        functools.partial(plan_kernel, n, per_dev, block_len, total // REQS),
        out_shape=(
            jax.ShapeDtypeStruct((1, slots), jnp.int32),
            jax.ShapeDtypeStruct((1, per_dev), jnp.int32),
            jax.ShapeDtypeStruct((1, per_dev * block_len), jnp.int32),
        ),
        in_specs=[vmem, vmem, pl.BlockSpec(memory_space=pltpu.SMEM)],
        out_specs=(vmem, vmem, vmem),
        name="plan",
    )(src_blocks.reshape(1, total), dst_blocks.reshape(1, total), lengths)


def place_kernel(index, arrived, attn, placed, result, sems, attn_sem):
    cap = arrived.shape[1]

    def write(i):
        at = index[0, i]
        return pltpu.make_async_copy(
            arrived.at[at // cap, lax.rem(at, cap)], placed.at[i], sems.at[i]
        )

    def loop(body):
        lax.fori_loop(0, placed.shape[0], lambda i, c: (body(i), c)[1], 0)

    attn_out = pltpu.make_async_copy(attn, result, attn_sem.at[0])
    loop(lambda i: write(i).start())
    attn_out.start()
    loop(lambda i: write(i).wait())
    attn_out.wait()


def place(arrived, attn, index):
    count = index.shape[1]
    shape = (count,) + arrived.shape[2:]
    dma = pltpu.SemaphoreType.DMA
    hbm = pl.BlockSpec(memory_space=pl.ANY)
    vmem = pl.BlockSpec(memory_space=pltpu.VMEM)
    return pl.pallas_call(
        place_kernel,
        out_shape=(
            jax.ShapeDtypeStruct(shape, arrived.dtype),
            jax.ShapeDtypeStruct(attn.shape, attn.dtype),
        ),
        in_specs=[pl.BlockSpec(memory_space=pltpu.SMEM), vmem, vmem],
        out_specs=(hbm, hbm),
        scratch_shapes=[
            dma((count,)),
            dma((1,)),
        ],
        compiler_params=pltpu.CompilerParams(vmem_limit_bytes=16 * 1024 * 1024),
        name="place",
    )(index, arrived, attn)


def split_bf16(value):
    high = value.astype(jnp.bfloat16)
    low = (value - high.astype(jnp.float32)).astype(jnp.bfloat16)
    return high, low


def dot(a, b, b_dim):
    return lax.dot_general(
        a, b, (((1,), (b_dim,)), ((), ())), preferred_element_type=jnp.float32
    )


def exchange_kernel(
    n,
    groups,
    halves,
    send_index,
    cache,
    queries,
    fresh_keys,
    fresh_values,
    token_request,
    arrived,
    result,
    outgoing,
    fresh_rows,
    fresh_bias,
    acc,
    acc_in,
    stat,
    stat_in,
    stat_cols,
    block_send,
    block_recv,
    pair_send,
    pair_recv,
    own_sem,
):
    me = lax.axis_index("ctx")
    blocks, layers, _, block_len, _ = cache.shape
    tokens = blocks * block_len
    cap = outgoing.shape[1]
    rows = acc.shape[3]
    stages = n.bit_length() - 1
    width = rows * halves

    def loop(start, stop, body):
        lax.fori_loop(start, stop, lambda k, c: (body(k), c)[1], 0)

    def peer(k):
        return lax.rem(me + k, n)

    def place_of(to):
        return sum(to // 2**j % 2 * (n // 2 ** (j + 1)) for j in range(stages))

    def send(src, dst, send_sem, recv_sem, device):
        return pltpu.make_async_remote_copy(
            src_ref=src,
            dst_ref=dst,
            send_sem=send_sem,
            recv_sem=recv_sem,
            device_id={"ctx": device},
            device_id_type=MESH,
        )

    barrier = pltpu.get_barrier_semaphore()
    loop(
        1,
        n,
        lambda k: pl.semaphore_signal(
            barrier, 1, device_id={"ctx": peer(k)}, device_id_type=MESH
        ),
    )
    pl.semaphore_wait(barrier, n - 1)

    def block_copy(k):
        return send(
            outgoing.at[peer(k)], arrived.at[me], block_send.at[k], block_recv.at[k], peer(k)
        )

    def fill(to):
        for c in range(cap):
            outgoing[to, c] = cache[send_index[0, to * cap + c]]

    def shift(i):
        j = i // 2
        odd = lax.rem(j, 2)
        far = n // 2 + odd * (j + 1) // 2 - (1 - odd) * (j // 2)
        near = (1 - odd) * (1 + j // 2) + odd * (n - (j + 1) // 2)
        pick = lax.rem(i, 2)
        return (1 - pick) * far + pick * near

    def send_blocks(i):
        k = shift(i)
        fill(peer(k))
        block_copy(k).start()

    rest = n // 2
    windows = [0, n // 4] + [
        rest + (n - 1 - rest) * j // stages for j in range(stages + 1)
    ]

    def send_window(w):
        loop(windows[w], windows[w + 1], send_blocks)

    send_window(0)
    fill(me)
    own_copy = pltpu.make_async_copy(outgoing.at[me], arrived.at[me], own_sem.at[0])
    own_copy.start()

    steps = queries.shape[0]
    heads = rows // steps
    fresh = steps * REQS
    for which, value in ((0, fresh_keys), (1, fresh_values)):
        for layer in range(layers):
            parts = [value[u, layer].astype(jnp.float32) for u in range(steps)]
            parts.append(jnp.zeros((fresh_rows.shape[2] - fresh, KVH * HD), jnp.float32))
            fresh_rows[which, layer] = jnp.concatenate(parts, axis=0).astype(jnp.bfloat16)
    bias_shape = (width, fresh_rows.shape[2])
    row = lax.broadcasted_iota(jnp.int32, bias_shape, 0)
    col = lax.broadcasted_iota(jnp.int32, bias_shape, 1)
    for h in range(1, halves):
        row = jnp.where(row >= rows, row - rows, row)
    row_step = sum((row >= heads * j).astype(jnp.int32) for j in range(1, steps))
    col_step = sum((col >= REQS * j).astype(jnp.int32) for j in range(1, steps))
    col_request = col - REQS * col_step
    usable = (col_step <= row_step) & (col < fresh) & (me == 0)
    for r in range(REQS):
        fresh_bias[r * width : (r + 1) * width] = jnp.where(
            usable & (col_request == r), 0.0, NEG_BIG
        )

    stat_cols[...] = jnp.zeros_like(stat_cols)
    lane = lax.broadcasted_iota(jnp.int32, (1, HD), 1)

    def query_rows(layer, g):
        span = pl.ds(pl.multiple_of(g * QPG * HD, QPG * HD), QPG * HD)
        parts = [
            queries[step, layer, :, span].astype(jnp.float32).reshape(REQS, QPG, HD)
            for step in range(steps)
        ]
        ordered = [
            parts[step][r, h * heads : (h + 1) * heads]
            for r in range(REQS)
            for h in range(halves)
            for step in range(steps)
        ]
        return jnp.concatenate(ordered, axis=0).astype(jnp.bfloat16)

    def head(g):
        cols = pl.ds(pl.multiple_of(g * HD, HD), HD)
        for layer in range(layers):
            q = query_rows(layer, g)
            k_cache = cache[:, layer, 0, :, cols].reshape(tokens, HD)
            v_cache = cache[:, layer, 1, :, cols].reshape(tokens, HD)
            k_new = fresh_rows[0, layer, :, cols]
            v_new = fresh_rows[1, layer, :, cols]
            scores = dot(q, k_cache, 1) * (HD**-0.5)
            new_scores = dot(q, k_new, 1) * (HD**-0.5)
            for r in range(REQS):
                part = slice(r * width, (r + 1) * width)
                live = jnp.where(token_request[...] == r, 0.0, NEG_BIG)
                s = scores[part] + live
                s_new = new_scores[part] + fresh_bias[part]
                top = jnp.maximum(
                    jnp.max(s, axis=1, keepdims=True), jnp.max(s_new, axis=1, keepdims=True)
                )
                w = jnp.exp(s - top)
                w_new = jnp.exp(s_new - top)
                total = jnp.sum(w, axis=1, keepdims=True) + jnp.sum(w_new, axis=1, keepdims=True)
                big, small = split_bf16(w)
                new_big, new_small = split_bf16(w_new)
                sums = (
                    dot(big, v_cache, 0)
                    + dot(small, v_cache, 0)
                    + dot(new_big, v_new, 0)
                    + dot(new_small, v_new, 0)
                )
                for h in range(halves):
                    chunk = (r * KVH + g) * halves + h
                    at = place_of(chunk // groups)
                    acc[at, chunk % groups, layer] = sums[h * rows : (h + 1) * rows]
                at = g * STAT_ROWS + layer
                now = stat_cols[part]
                now = jnp.where(lane == at, top, now)
                stat_cols[part] = jnp.where(lane == at + layers, total, now)

    span = windows[2] - windows[1]
    stops = KVH // 2

    def head_pair(i):
        loop(2 * i, 2 * i + 2, head)
        loop(
            windows[1] + lax.div(span * i, stops),
            windows[1] + lax.div(span * (i + 1), stops),
            send_blocks,
        )

    loop(0, stops, head_pair)

    pad = jnp.zeros((HD - rows, HD), jnp.float32)
    for r in range(REQS):
        for h in range(halves):
            start = (r * halves + h) * rows
            turned = jnp.concatenate([stat_cols[start : start + rows], pad], axis=0).T
            for g in range(KVH):
                chunk = (r * KVH + g) * halves + h
                stat[place_of(chunk // groups), chunk % groups] = turned[
                    g * STAT_ROWS : (g + 1) * STAT_ROWS
                ]

    def columns(factors):
        filler = jnp.zeros((HD - factors.shape[0], HD), jnp.float32)
        return jnp.concatenate([factors, filler], axis=0).T

    def join(acc_own, stat_own, acc_new, stat_new):
        for gi in range(groups):
            a, b = stat_own[gi], stat_new[gi]
            top = jnp.maximum(a[:layers], b[:layers])
            keep = jnp.exp(a[:layers] - top)
            add = jnp.exp(b[:layers] - top)
            total = a[layers : 2 * layers] * keep + b[layers : 2 * layers] * add
            filler = jnp.zeros((STAT_ROWS - 2 * layers, HD), jnp.float32)
            stat_own[gi] = jnp.concatenate([top, total, filler], axis=0)
            factor = columns(jnp.concatenate([keep, add], axis=0))
            for layer in range(layers):
                acc_own[gi, layer] = (
                    acc_own[gi, layer] * factor[:rows, layer : layer + 1]
                    + acc_new[gi, layer] * factor[:rows, layers + layer : layers + layer + 1]
                )

    base = 0
    for stage in range(stages):
        half = n // 2 ** (stage + 1)
        bit = lax.rem(me // 2**stage, 2)
        partner = me + 2**stage * (1 - 2 * bit)
        keep, give = base + bit * half, base + (1 - bit) * half
        at = n - 2 * half
        copies = [
            send(
                src.at[pl.ds(give, half)],
                dst.at[pl.ds(at, half)],
                pair_send.at[i, stage],
                pair_recv.at[i, stage],
                partner,
            )
            for i, (src, dst) in enumerate(((stat, stat_in), (acc, acc_in)))
        ]
        for copy in copies:
            copy.start()
        loop(windows[2 + stage], windows[3 + stage], send_blocks)
        for copy in copies:
            copy.wait()
        loop(
            0,
            half,
            lambda i, keep=keep, at=at: join(
                acc.at[keep + i], stat.at[keep + i], acc_in.at[at + i], stat_in.at[at + i]
            ),
        )
        base = keep

    share = rows // result.shape[0]
    for gi in range(groups):
        totals = stat[base, gi, layers : 2 * layers]
        factor = columns(1.0 / totals)
        for layer in range(layers):
            out = acc[base, gi, layer] * factor[:rows, layer : layer + 1]
            for step in range(result.shape[0]):
                result[step, layer, gi * share : (gi + 1) * share, :] = out[
                    step * share : (step + 1) * share
                ]

    own_copy.wait()
    loop(1, n, lambda k: block_copy(k).wait())


def exchange(n, cap, send_index, cache, queries, fresh_keys, fresh_values, token_request):
    steps, layers, requests, _ = queries.shape
    share = requests * KVH * QPG // n
    groups = max(share // QPG, 1)
    halves = max(QPG // share, 1)
    heads = QPG // halves
    rows = steps * heads
    fresh_pad = -(-steps * requests // 16) * 16
    stages = n.bit_length() - 1
    block = cache.shape[1:]
    piece = (groups, layers, rows, HD)
    note = (groups, STAT_ROWS, HD)
    vmem = pl.BlockSpec(memory_space=pltpu.VMEM)
    smem = pl.BlockSpec(memory_space=pltpu.SMEM)
    hbm = pl.BlockSpec(memory_space=pl.ANY)
    dma = pltpu.SemaphoreType.DMA
    f32 = jnp.float32
    return pl.pallas_call(
        functools.partial(exchange_kernel, n, groups, halves),
        out_shape=(
            jax.ShapeDtypeStruct((n, cap) + block, cache.dtype),
            jax.ShapeDtypeStruct((steps, layers, share, HD), f32),
        ),
        in_specs=[smem] + [vmem] * 5,
        out_specs=(hbm, vmem),
        scratch_shapes=[
            pltpu.VMEM((n, cap) + block, cache.dtype),
            pltpu.VMEM((2, layers, fresh_pad, KVH * HD), cache.dtype),
            pltpu.VMEM((requests * halves * rows, fresh_pad), f32),
            pltpu.VMEM((n,) + piece, f32),
            pltpu.VMEM((n - 1,) + piece, f32),
            pltpu.VMEM((n,) + note, f32),
            pltpu.VMEM((n - 1,) + note, f32),
            pltpu.VMEM((requests * halves * rows, HD), f32),
            dma((n,)),
            dma((n,)),
            dma((2, stages)),
            dma((2, stages)),
            dma((1,)),
        ],
        compiler_params=pltpu.CompilerParams(
            collective_id=0, has_side_effects=True, vmem_limit_bytes=32 * 1024 * 1024
        ),
        name="exchange",
    )(send_index, cache, queries, fresh_keys, fresh_values, token_request)


def local(src_cache, src_blocks, dst_blocks, ctx_lengths, queries, new_keys, new_values):
    n = lax.axis_size("ctx")
    per_dev, _, _, block_len, _ = src_cache.shape
    cap = (per_dev + n - 1) // n
    send_index, take_index, token_request = plan(
        n, per_dev, block_len, src_blocks, dst_blocks, ctx_lengths
    )
    arrived, attn = exchange(
        n, cap, send_index, src_cache, queries, new_keys, new_values, token_request
    )
    return place(arrived, attn, take_index)


def solution(mesh):
    in_specs = (
        P(("groups", "ctx"), None, None, None, None),
        P("groups"),
        P("groups"),
        P("groups"),
        P(None, None, "groups", None),
        P(None, None, "groups", None),
        P(None, None, "groups", None),
    )
    out_specs = (
        P(("groups", "ctx"), None, None, None, None),
        P(None, None, ("groups", "ctx"), None),
    )
    return jax.shard_map(local, mesh=mesh, in_specs=in_specs, out_specs=out_specs, check_vma=False)
```

```python
import functools

import jax
import jax.numpy as jnp
from jax import lax
from jax.experimental import pallas as pl
from jax.experimental.pallas import tpu as pltpu
from jax.sharding import PartitionSpec as P

KVH = 8
HD = 128
QPG = 16
REQS = 4

NEG_BIG = -1e30
STAT_ROWS = 8
MESH = pl.DeviceIdType.MESH


def over(value, by):
    assert by & (by - 1) == 0
    return lax.shift_right_logical(value, by.bit_length() - 1)


def plan(n, me, per_dev, block_len, src, dst, lengths, send_index, take_index, tokens_of):
    cap = (per_dev + n - 1) // n
    total = src.shape[1]
    per_request = total // REQS

    def iota(cols, axis):
        return lax.broadcasted_iota(jnp.int32, (per_dev, cols), axis)

    lane = iota(total, 1)
    own = lane == iota(total, 0) + me * per_dev
    small_lane, small_sub = iota(per_dev, 1), iota(per_dev, 0)

    def column(mask, row):
        return jnp.sum(jnp.where(mask, row, 0), axis=1, keepdims=True)

    def as_row(col):
        return jnp.sum(jnp.where(small_lane == small_sub, col, 0), axis=0, keepdims=True)

    src_ids = column(own, src)
    target = over(column(src_ids == dst, lane), per_dev)
    same = (target == as_row(target)) & (small_lane < small_sub)
    bucket = target * cap + column(same, 1)
    slots = send_index.shape[1]
    filled = jnp.where(bucket == iota(slots, 1), iota(slots, 0), 0)
    send_index[...] = jnp.sum(filled, axis=0, keepdims=True)

    root = column(column(own, dst) == src, lane)
    owner = over(root, per_dev)
    earlier = (owner == as_row(owner)) & (as_row(root) < root)
    take_index[...] = as_row(owner * cap + column(earlier, 1))

    token, block = iota(per_dev * block_len, 1), iota(per_dev * block_len, 0)
    holds = over(token, block_len) == block
    ids = jnp.sum(jnp.where(holds, src_ids, 0), axis=0, keepdims=True)
    request = over(ids, per_request)
    at = (ids - request * per_request) * block_len + (token[:1] & (block_len - 1))
    limit = jnp.zeros_like(at)
    for r in range(REQS):
        limit = jnp.where(request == r, lengths[r], limit)
    tokens_of[...] = jnp.where(at < limit, request, -1)


def place_kernel(
    index, arrived, attn, placed, result, held, held_attn, in_sems, out_sems, attn_sems
):
    cap = arrived.shape[1]

    def read(i):
        at = index[0, i]
        return pltpu.make_async_copy(
            arrived.at[at // cap, lax.rem(at, cap)], held.at[i], in_sems.at[i]
        )

    def write(i):
        return pltpu.make_async_copy(held.at[i], placed.at[i], out_sems.at[i])

    def loop(body):
        lax.fori_loop(0, held.shape[0], lambda i, c: (body(i), c)[1], 0)

    attn_in = pltpu.make_async_copy(attn, held_attn, attn_sems.at[0])
    attn_out = pltpu.make_async_copy(held_attn, result, attn_sems.at[1])
    attn_in.start()
    loop(lambda i: read(i).start())
    attn_in.wait()
    attn_out.start()
    loop(lambda i: (read(i).wait(), write(i).start()))
    loop(lambda i: write(i).wait())
    attn_out.wait()


def place(arrived, attn, index):
    count = index.shape[1]
    shape = (count,) + arrived.shape[2:]
    dma = pltpu.SemaphoreType.DMA
    hbm = pl.BlockSpec(memory_space=pltpu.HBM)
    return pl.pallas_call(
        place_kernel,
        out_shape=(
            jax.ShapeDtypeStruct(shape, arrived.dtype),
            jax.ShapeDtypeStruct(attn.shape, attn.dtype),
        ),
        in_specs=[pl.BlockSpec(memory_space=pltpu.SMEM), hbm, hbm],
        out_specs=(hbm, hbm),
        scratch_shapes=[
            pltpu.VMEM(shape, arrived.dtype),
            pltpu.VMEM(attn.shape, attn.dtype),
            dma((count,)),
            dma((count,)),
            dma((2,)),
        ],
        compiler_params=pltpu.CompilerParams(vmem_limit_bytes=60 * 1024 * 1024),
        name="place",
    )(index, arrived, attn)


def split_bf16(value):
    high = value.astype(jnp.bfloat16)
    low = (value - high.astype(jnp.float32)).astype(jnp.bfloat16)
    return high, low


def dot(a, b, b_dim):
    return lax.dot_general(
        a, b, (((1,), (b_dim,)), ((), ())), preferred_element_type=jnp.float32
    )


def exchange_kernel(
    n,
    groups,
    halves,
    lengths,
    *refs,
):
    *sources, arrived, result, take_index = refs[:9]
    cache, queries, fresh_keys, fresh_values, src_blocks, dst_blocks = loaded = refs[9:15]
    kernel_body(n, groups, halves, lengths, sources, loaded, arrived, result, take_index, *refs[15:])


def kernel_body(
    n,
    groups,
    halves,
    lengths,
    sources,
    loaded,
    arrived,
    result,
    take_index,
    outgoing,
    send_vector,
    send_index,
    token_request,
    fresh_rows,
    fresh_bias,
    acc,
    acc_in,
    stat,
    stat_in,
    stat_cols,
    block_send,
    block_recv,
    pair_send,
    pair_recv,
    own_sem,
):
    cache, queries, fresh_keys, fresh_values, src_blocks, dst_blocks = loaded
    me = lax.axis_index("ctx")
    blocks, layers, _, block_len, _ = cache.shape
    tokens = blocks * block_len
    cap = outgoing.shape[1]
    rows = acc.shape[3]
    stages = n.bit_length() - 1
    width = rows * halves

    def loop(start, stop, body):
        lax.fori_loop(start, stop, lambda k, c: (body(k), c)[1], 0)

    def peer(k):
        return lax.rem(me + k, n)

    def place_of(to):
        return sum(to // 2**j % 2 * (n // 2 ** (j + 1)) for j in range(stages))

    def send(src, dst, send_sem, recv_sem, device):
        return pltpu.make_async_remote_copy(
            src_ref=src,
            dst_ref=dst,
            send_sem=send_sem,
            recv_sem=recv_sem,
            device_id={"ctx": device},
            device_id_type=MESH,
        )

    loads = [
        pltpu.make_async_copy(src, dst, own_sem.at[1 + i])
        for i, (src, dst) in enumerate(zip(sources, loaded))
    ]
    for load in loads[::-1]:
        load.start()

    barrier = pltpu.get_barrier_semaphore()
    loop(
        1,
        n,
        lambda k: pl.semaphore_signal(
            barrier, 1, device_id={"ctx": peer(k)}, device_id_type=MESH
        ),
    )
    loads[4].wait()
    loads[5].wait()
    plan(
        n,
        me,
        blocks,
        block_len,
        src_blocks[...],
        dst_blocks[...],
        lengths,
        send_vector,
        take_index,
        token_request,
    )
    index_copy = pltpu.make_async_copy(send_vector, send_index, own_sem.at[7])
    index_copy.start()
    pl.semaphore_wait(barrier, n - 1)
    index_copy.wait()
    loads[0].wait()

    def block_copy(k):
        return send(
            outgoing.at[peer(k)], arrived.at[me], block_send.at[k], block_recv.at[k], peer(k)
        )

    def fill(to):
        for c in range(cap):
            outgoing[to, c] = cache[send_index[0, to * cap + c]]

    def shift(i):
        j = i // 2
        odd = lax.rem(j, 2)
        far = n // 2 + odd * (j + 1) // 2 - (1 - odd) * (j // 2)
        near = (1 - odd) * (1 + j // 2) + odd * (n - (j + 1) // 2)
        pick = lax.rem(i, 2)
        return (1 - pick) * far + pick * near

    def send_blocks(i):
        k = shift(i)
        fill(peer(k))
        block_copy(k).start()

    rest = n // 2
    windows = [0, n // 4] + [
        rest + (n - 1 - rest) * j // stages for j in range(stages + 1)
    ]

    def send_window(w):
        loop(windows[w], windows[w + 1], send_blocks)

    send_window(0)
    fill(me)
    own_copy = pltpu.make_async_copy(outgoing.at[me], arrived.at[me], own_sem.at[0])
    own_copy.start()
    for load in loads[1:4]:
        load.wait()

    steps = queries.shape[0]
    heads = rows // steps
    fresh = steps * REQS
    for which, value in ((0, fresh_keys), (1, fresh_values)):
        for layer in range(layers):
            parts = [value[u, layer].astype(jnp.float32) for u in range(steps)]
            parts.append(jnp.zeros((fresh_rows.shape[2] - fresh, KVH * HD), jnp.float32))
            fresh_rows[which, layer] = jnp.concatenate(parts, axis=0).astype(jnp.bfloat16)
    bias_shape = (width, fresh_rows.shape[2])
    row = lax.broadcasted_iota(jnp.int32, bias_shape, 0)
    col = lax.broadcasted_iota(jnp.int32, bias_shape, 1)
    for h in range(1, halves):
        row = jnp.where(row >= rows, row - rows, row)
    row_step = sum((row >= heads * j).astype(jnp.int32) for j in range(1, steps))
    col_step = sum((col >= REQS * j).astype(jnp.int32) for j in range(1, steps))
    col_request = col - REQS * col_step
    usable = (col_step <= row_step) & (col < fresh) & (me == 0)
    for r in range(REQS):
        fresh_bias[r * width : (r + 1) * width] = jnp.where(
            usable & (col_request == r), 0.0, NEG_BIG
        )

    stat_cols[...] = jnp.zeros_like(stat_cols)
    lane = lax.broadcasted_iota(jnp.int32, (1, HD), 1)

    def query_rows(layer, g):
        span = pl.ds(pl.multiple_of(g * QPG * HD, QPG * HD), QPG * HD)
        parts = [
            queries[step, layer, :, span].astype(jnp.float32).reshape(REQS, QPG, HD)
            for step in range(steps)
        ]
        ordered = [
            parts[step][r, h * heads : (h + 1) * heads]
            for r in range(REQS)
            for h in range(halves)
            for step in range(steps)
        ]
        return jnp.concatenate(ordered, axis=0).astype(jnp.bfloat16)

    def head(g):
        cols = pl.ds(pl.multiple_of(g * HD, HD), HD)
        for layer in range(layers):
            q = query_rows(layer, g)
            k_cache = cache[:, layer, 0, :, cols].reshape(tokens, HD)
            v_cache = cache[:, layer, 1, :, cols].reshape(tokens, HD)
            k_new = fresh_rows[0, layer, :, cols]
            v_new = fresh_rows[1, layer, :, cols]
            scores = dot(q, k_cache, 1) * (HD**-0.5)
            new_scores = dot(q, k_new, 1) * (HD**-0.5)
            for r in range(REQS):
                part = slice(r * width, (r + 1) * width)
                live = jnp.where(token_request[...] == r, 0.0, NEG_BIG)
                s = scores[part] + live
                s_new = new_scores[part] + fresh_bias[part]
                top = jnp.maximum(
                    jnp.max(s, axis=1, keepdims=True), jnp.max(s_new, axis=1, keepdims=True)
                )
                w = jnp.exp(s - top)
                w_new = jnp.exp(s_new - top)
                total = jnp.sum(w, axis=1, keepdims=True) + jnp.sum(w_new, axis=1, keepdims=True)
                big, small = split_bf16(w)
                new_big, new_small = split_bf16(w_new)
                sums = (
                    dot(big, v_cache, 0)
                    + dot(small, v_cache, 0)
                    + dot(new_big, v_new, 0)
                    + dot(new_small, v_new, 0)
                )
                for h in range(halves):
                    chunk = (r * KVH + g) * halves + h
                    at = place_of(chunk // groups)
                    acc[at, chunk % groups, layer] = sums[h * rows : (h + 1) * rows]
                at = g * STAT_ROWS + layer
                now = stat_cols[part]
                now = jnp.where(lane == at, top, now)
                stat_cols[part] = jnp.where(lane == at + layers, total, now)

    span = windows[2] - windows[1]
    stops = KVH // 2

    def head_pair(i):
        loop(2 * i, 2 * i + 2, head)
        loop(
            windows[1] + lax.div(span * i, stops),
            windows[1] + lax.div(span * (i + 1), stops),
            send_blocks,
        )

    loop(0, stops, head_pair)

    pad = jnp.zeros((HD - rows, HD), jnp.float32)
    for r in range(REQS):
        for h in range(halves):
            start = (r * halves + h) * rows
            turned = jnp.concatenate([stat_cols[start : start + rows], pad], axis=0).T
            for g in range(KVH):
                chunk = (r * KVH + g) * halves + h
                stat[place_of(chunk // groups), chunk % groups] = turned[
                    g * STAT_ROWS : (g + 1) * STAT_ROWS
                ]

    def columns(factors):
        filler = jnp.zeros((HD - factors.shape[0], HD), jnp.float32)
        return jnp.concatenate([factors, filler], axis=0).T

    def join(acc_own, stat_own, acc_new, stat_new):
        for gi in range(groups):
            a, b = stat_own[gi], stat_new[gi]
            top = jnp.maximum(a[:layers], b[:layers])
            keep = jnp.exp(a[:layers] - top)
            add = jnp.exp(b[:layers] - top)
            total = a[layers : 2 * layers] * keep + b[layers : 2 * layers] * add
            filler = jnp.zeros((STAT_ROWS - 2 * layers, HD), jnp.float32)
            stat_own[gi] = jnp.concatenate([top, total, filler], axis=0)
            factor = columns(jnp.concatenate([keep, add], axis=0))
            for layer in range(layers):
                acc_own[gi, layer] = (
                    acc_own[gi, layer] * factor[:rows, layer : layer + 1]
                    + acc_new[gi, layer] * factor[:rows, layers + layer : layers + layer + 1]
                )

    base = 0
    for stage in range(stages):
        half = n // 2 ** (stage + 1)
        bit = lax.rem(me // 2**stage, 2)
        partner = me + 2**stage * (1 - 2 * bit)
        keep, give = base + bit * half, base + (1 - bit) * half
        at = n - 2 * half
        copies = [
            send(
                src.at[pl.ds(give, half)],
                dst.at[pl.ds(at, half)],
                pair_send.at[i, stage],
                pair_recv.at[i, stage],
                partner,
            )
            for i, (src, dst) in enumerate(((stat, stat_in), (acc, acc_in)))
        ]
        for copy in copies:
            copy.start()
        loop(windows[2 + stage], windows[3 + stage], send_blocks)
        for copy in copies:
            copy.wait()
        loop(
            0,
            half,
            lambda i, keep=keep, at=at: join(
                acc.at[keep + i], stat.at[keep + i], acc_in.at[at + i], stat_in.at[at + i]
            ),
        )
        base = keep

    share = rows // result.shape[0]
    for gi in range(groups):
        totals = stat[base, gi, layers : 2 * layers]
        factor = columns(1.0 / totals)
        for layer in range(layers):
            out = acc[base, gi, layer] * factor[:rows, layer : layer + 1]
            for step in range(result.shape[0]):
                result[step, layer, gi * share : (gi + 1) * share, :] = out[
                    step * share : (step + 1) * share
                ]

    own_copy.wait()
    loop(1, n, lambda k: block_copy(k).wait())


def exchange(n, cap, lengths, *arrays):
    cache, queries = arrays[:2]
    steps, layers, requests, _ = queries.shape
    share = requests * KVH * QPG // n
    groups = max(share // QPG, 1)
    halves = max(QPG // share, 1)
    heads = QPG // halves
    rows = steps * heads
    fresh_pad = -(-steps * requests // 16) * 16
    stages = n.bit_length() - 1
    block = cache.shape[1:]
    per_dev, block_len = cache.shape[0], cache.shape[3]
    slots = -(-n * cap // HD) * HD
    piece = (groups, layers, rows, HD)
    note = (groups, STAT_ROWS, HD)
    vmem = pl.BlockSpec(memory_space=pltpu.VMEM)
    smem = pl.BlockSpec(memory_space=pltpu.SMEM)
    hbm = pl.BlockSpec(memory_space=pl.ANY)
    dma = pltpu.SemaphoreType.DMA
    f32 = jnp.float32
    return pl.pallas_call(
        functools.partial(exchange_kernel, n, groups, halves),
        out_shape=(
            jax.ShapeDtypeStruct((n, cap) + block, cache.dtype),
            jax.ShapeDtypeStruct((steps, layers, share, HD), f32),
            jax.ShapeDtypeStruct((1, per_dev), jnp.int32),
        ),
        in_specs=[smem] + [pl.BlockSpec(memory_space=pltpu.HBM)] * len(arrays),
        out_specs=(hbm, vmem, vmem),
        scratch_shapes=[pltpu.VMEM(array.shape, array.dtype) for array in arrays]
        + [
            pltpu.VMEM((n, cap) + block, cache.dtype),
            pltpu.VMEM((1, slots), jnp.int32),
            pltpu.SMEM((1, slots), jnp.int32),
            pltpu.VMEM((1, per_dev * block_len), jnp.int32),
            pltpu.VMEM((2, layers, fresh_pad, KVH * HD), cache.dtype),
            pltpu.VMEM((requests * halves * rows, fresh_pad), f32),
            pltpu.VMEM((n,) + piece, f32),
            pltpu.VMEM((n - 1,) + piece, f32),
            pltpu.VMEM((n,) + note, f32),
            pltpu.VMEM((n - 1,) + note, f32),
            pltpu.VMEM((requests * halves * rows, HD), f32),
            dma((n,)),
            dma((n,)),
            dma((2, stages)),
            dma((2, stages)),
            dma((8,)),
        ],
        compiler_params=pltpu.CompilerParams(
            collective_id=0, has_side_effects=True, vmem_limit_bytes=60 * 1024 * 1024
        ),
        name="exchange",
    )(lengths, *arrays)


def local(src_cache, src_blocks, dst_blocks, ctx_lengths, queries, new_keys, new_values):
    n = lax.axis_size("ctx")
    cap = (src_cache.shape[0] + n - 1) // n
    tables = [blocks.reshape(1, -1) for blocks in (src_blocks, dst_blocks)]
    arrived, attn, take_index = exchange(
        n, cap, ctx_lengths, src_cache, queries, new_keys, new_values, *tables
    )
    return place(arrived, attn, take_index)


def solution(mesh):
    in_specs = (
        P(("groups", "ctx"), None, None, None, None),
        P("groups"),
        P("groups"),
        P("groups"),
        P(None, None, "groups", None),
        P(None, None, "groups", None),
        P(None, None, "groups", None),
    )
    out_specs = (
        P(("groups", "ctx"), None, None, None, None),
        P(None, None, ("groups", "ctx"), None),
    )
    return jax.shard_map(local, mesh=mesh, in_specs=in_specs, out_specs=out_specs, check_vma=False)
```

```python
import functools

import jax
import jax.numpy as jnp
from jax import lax
from jax.experimental import pallas as pl
from jax.experimental.pallas import tpu as pltpu
from jax.sharding import PartitionSpec as P

KVH = 8
HD = 128
QPG = 16
REQS = 4

NEG_BIG = -1e30
STAT_ROWS = 8
LEVELS = 32767.0
TINY = 1e-30
MESH = pl.DeviceIdType.MESH


def over(value, by):
    assert by & (by - 1) == 0
    return lax.shift_right_logical(value, by.bit_length() - 1)


def plan(n, me, per_dev, block_len, src, dst, lengths, send_index, take_index, tokens_of):
    cap = (per_dev + n - 1) // n
    total = src.shape[1]
    per_request = total // REQS

    def iota(cols, axis):
        return lax.broadcasted_iota(jnp.int32, (per_dev, cols), axis)

    lane = iota(total, 1)
    own = lane == iota(total, 0) + me * per_dev
    small_lane, small_sub = iota(per_dev, 1), iota(per_dev, 0)

    def column(mask, row):
        return jnp.sum(jnp.where(mask, row, 0), axis=1, keepdims=True)

    def as_row(col):
        return jnp.sum(jnp.where(small_lane == small_sub, col, 0), axis=0, keepdims=True)

    src_ids = column(own, src)
    target = over(column(src_ids == dst, lane), per_dev)
    same = (target == as_row(target)) & (small_lane < small_sub)
    bucket = target * cap + column(same, 1)
    slots = send_index.shape[1]
    filled = jnp.where(bucket == iota(slots, 1), iota(slots, 0), 0)
    send_index[...] = jnp.sum(filled, axis=0, keepdims=True)

    root = column(column(own, dst) == src, lane)
    owner = over(root, per_dev)
    earlier = (owner == as_row(owner)) & (as_row(root) < root)
    take_index[...] = as_row(owner * cap + column(earlier, 1))

    token, block = iota(per_dev * block_len, 1), iota(per_dev * block_len, 0)
    holds = over(token, block_len) == block
    ids = jnp.sum(jnp.where(holds, src_ids, 0), axis=0, keepdims=True)
    request = over(ids, per_request)
    at = (ids - request * per_request) * block_len + (token[:1] & (block_len - 1))
    limit = jnp.zeros_like(at)
    for r in range(REQS):
        limit = jnp.where(request == r, lengths[r], limit)
    tokens_of[...] = jnp.where(at < limit, request, -1)


def place_kernel(
    index, arrived, attn, placed, result, held, held_attn, in_sems, out_sems, attn_sems
):
    cap = arrived.shape[1]

    def read(i):
        at = index[0, i]
        return pltpu.make_async_copy(
            arrived.at[at // cap, lax.rem(at, cap)], held.at[i], in_sems.at[i]
        )

    def write(i):
        return pltpu.make_async_copy(held.at[i], placed.at[i], out_sems.at[i])

    count = held.shape[0]
    window = min(8, count)

    def loop(start, stop, body):
        lax.fori_loop(start, stop, lambda i, c: (body(i), c)[1], 0)

    attn_in = pltpu.make_async_copy(attn, held_attn, attn_sems.at[0])
    attn_out = pltpu.make_async_copy(held_attn, result, attn_sems.at[1])
    attn_in.start()
    loop(0, window, lambda i: read(i).start())
    attn_in.wait()
    attn_out.start()
    loop(
        0,
        count - window,
        lambda i: (read(i).wait(), write(i).start(), read(i + window).start()),
    )
    loop(count - window, count, lambda i: (read(i).wait(), write(i).start()))
    loop(0, count, lambda i: write(i).wait())
    attn_out.wait()


def place(arrived, attn, index):
    count = index.shape[1]
    shape = (count,) + arrived.shape[2:]
    dma = pltpu.SemaphoreType.DMA
    hbm = pl.BlockSpec(memory_space=pltpu.HBM)
    return pl.pallas_call(
        place_kernel,
        out_shape=(
            jax.ShapeDtypeStruct(shape, arrived.dtype),
            jax.ShapeDtypeStruct(attn.shape, attn.dtype),
        ),
        in_specs=[pl.BlockSpec(memory_space=pltpu.SMEM), hbm, hbm],
        out_specs=(hbm, hbm),
        scratch_shapes=[
            pltpu.VMEM(shape, arrived.dtype),
            pltpu.VMEM(attn.shape, attn.dtype),
            dma((count,)),
            dma((count,)),
            dma((2,)),
        ],
        compiler_params=pltpu.CompilerParams(vmem_limit_bytes=60 * 1024 * 1024),
        name="place",
    )(index, arrived, attn)


def split_bf16(value):
    high = value.astype(jnp.bfloat16)
    low = (value - high.astype(jnp.float32)).astype(jnp.bfloat16)
    return high, low


def dot(a, b, b_dim):
    return lax.dot_general(
        a, b, (((1,), (b_dim,)), ((), ())), preferred_element_type=jnp.float32
    )


def exchange_kernel(
    n,
    groups,
    halves,
    lengths,
    *refs,
):
    *sources, arrived, result, take_index = refs[:9]
    cache, queries, fresh_keys, fresh_values, src_blocks, dst_blocks = loaded = refs[9:15]
    kernel_body(n, groups, halves, lengths, sources, loaded, arrived, result, take_index, *refs[15:])


def kernel_body(
    n,
    groups,
    halves,
    lengths,
    sources,
    loaded,
    arrived,
    result,
    take_index,
    outgoing,
    send_vector,
    send_index,
    token_request,
    fresh_rows,
    fresh_bias,
    acc,
    acc_in,
    coded,
    coded_in,
    stat,
    stat_in,
    stat_cols,
    block_send,
    block_recv,
    pair_send,
    pair_recv,
    own_sem,
):
    cache, queries, fresh_keys, fresh_values, src_blocks, dst_blocks = loaded
    me = lax.axis_index("ctx")
    blocks, layers, _, block_len, _ = cache.shape
    tokens = blocks * block_len
    cap = outgoing.shape[1]
    rows = acc.shape[3]
    stages = n.bit_length() - 1
    width = rows * halves

    def loop(start, stop, body):
        lax.fori_loop(start, stop, lambda k, c: (body(k), c)[1], 0)

    def peer(k):
        return lax.rem(me + k, n)

    def place_of(to):
        return sum(to // 2**j % 2 * (n // 2 ** (j + 1)) for j in range(stages))

    def send(src, dst, send_sem, recv_sem, device):
        return pltpu.make_async_remote_copy(
            src_ref=src,
            dst_ref=dst,
            send_sem=send_sem,
            recv_sem=recv_sem,
            device_id={"ctx": device},
            device_id_type=MESH,
        )

    loads = [
        pltpu.make_async_copy(src, dst, own_sem.at[1 + i])
        for i, (src, dst) in enumerate(zip(sources, loaded))
    ]
    for load in loads[::-1]:
        load.start()

    barrier = pltpu.get_barrier_semaphore()
    loop(
        1,
        n,
        lambda k: pl.semaphore_signal(
            barrier, 1, device_id={"ctx": peer(k)}, device_id_type=MESH
        ),
    )
    loads[4].wait()
    loads[5].wait()
    plan(
        n,
        me,
        blocks,
        block_len,
        src_blocks[...],
        dst_blocks[...],
        lengths,
        send_vector,
        take_index,
        token_request,
    )
    index_copy = pltpu.make_async_copy(send_vector, send_index, own_sem.at[7])
    index_copy.start()
    pl.semaphore_wait(barrier, n - 1)
    index_copy.wait()
    loads[0].wait()

    def block_copy(k):
        return send(
            outgoing.at[peer(k)], arrived.at[me], block_send.at[k], block_recv.at[k], peer(k)
        )

    def fill(to):
        for c in range(cap):
            outgoing[to, c] = cache[send_index[0, to * cap + c]]

    def shift(i):
        j = i // 2
        odd = lax.rem(j, 2)
        far = n // 2 + odd * (j + 1) // 2 - (1 - odd) * (j // 2)
        near = (1 - odd) * (1 + j // 2) + odd * (n - (j + 1) // 2)
        pick = lax.rem(i, 2)
        return (1 - pick) * far + pick * near

    def send_blocks(i):
        k = shift(i)
        fill(peer(k))
        block_copy(k).start()

    rest = n // 2
    windows = [0, n // 4] + [
        rest + (n - 1 - rest) * j // stages for j in range(stages + 1)
    ]

    def send_window(w):
        loop(windows[w], windows[w + 1], send_blocks)

    send_window(0)
    fill(me)
    own_copy = pltpu.make_async_copy(outgoing.at[me], arrived.at[me], own_sem.at[0])
    own_copy.start()
    for load in loads[1:4]:
        load.wait()

    steps = queries.shape[0]
    heads = rows // steps
    fresh = steps * REQS
    for which, value in ((0, fresh_keys), (1, fresh_values)):
        for layer in range(layers):
            parts = [value[u, layer].astype(jnp.float32) for u in range(steps)]
            parts.append(jnp.zeros((fresh_rows.shape[2] - fresh, KVH * HD), jnp.float32))
            fresh_rows[which, layer] = jnp.concatenate(parts, axis=0).astype(jnp.bfloat16)
    bias_shape = (width, fresh_rows.shape[2])
    row = lax.broadcasted_iota(jnp.int32, bias_shape, 0)
    col = lax.broadcasted_iota(jnp.int32, bias_shape, 1)
    for h in range(1, halves):
        row = jnp.where(row >= rows, row - rows, row)
    row_step = sum((row >= heads * j).astype(jnp.int32) for j in range(1, steps))
    col_step = sum((col >= REQS * j).astype(jnp.int32) for j in range(1, steps))
    col_request = col - REQS * col_step
    usable = (col_step <= row_step) & (col < fresh) & (me == 0)
    for r in range(REQS):
        fresh_bias[r * width : (r + 1) * width] = jnp.where(
            usable & (col_request == r), 0.0, NEG_BIG
        )

    stat_cols[...] = jnp.zeros_like(stat_cols)
    lane = lax.broadcasted_iota(jnp.int32, (1, HD), 1)

    def query_rows(layer, g):
        span = pl.ds(pl.multiple_of(g * QPG * HD, QPG * HD), QPG * HD)
        parts = [
            queries[step, layer, :, span].astype(jnp.float32).reshape(REQS, QPG, HD)
            for step in range(steps)
        ]
        ordered = [
            parts[step][r, h * heads : (h + 1) * heads]
            for r in range(REQS)
            for h in range(halves)
            for step in range(steps)
        ]
        return jnp.concatenate(ordered, axis=0).astype(jnp.bfloat16)

    def head(g):
        cols = pl.ds(pl.multiple_of(g * HD, HD), HD)
        for layer in range(layers):
            q = query_rows(layer, g)
            k_cache = cache[:, layer, 0, :, cols].reshape(tokens, HD)
            v_cache = cache[:, layer, 1, :, cols].reshape(tokens, HD)
            k_new = fresh_rows[0, layer, :, cols]
            v_new = fresh_rows[1, layer, :, cols]
            scores = dot(q, k_cache, 1) * (HD**-0.5)
            new_scores = dot(q, k_new, 1) * (HD**-0.5)
            for r in range(REQS):
                part = slice(r * width, (r + 1) * width)
                live = jnp.where(token_request[...] == r, 0.0, NEG_BIG)
                s = scores[part] + live
                s_new = new_scores[part] + fresh_bias[part]
                top = jnp.maximum(
                    jnp.max(s, axis=1, keepdims=True), jnp.max(s_new, axis=1, keepdims=True)
                )
                w = jnp.exp(s - top)
                w_new = jnp.exp(s_new - top)
                total = jnp.sum(w, axis=1, keepdims=True) + jnp.sum(w_new, axis=1, keepdims=True)
                big, small = split_bf16(w)
                new_big, new_small = split_bf16(w_new)
                sums = (
                    dot(big, v_cache, 0)
                    + dot(small, v_cache, 0)
                    + dot(new_big, v_new, 0)
                    + dot(new_small, v_new, 0)
                )
                for h in range(halves):
                    chunk = (r * KVH + g) * halves + h
                    at = place_of(chunk // groups)
                    acc[at, chunk % groups, layer] = sums[h * rows : (h + 1) * rows]
                at = g * STAT_ROWS + layer
                now = stat_cols[part]
                now = jnp.where(lane == at, top, now)
                stat_cols[part] = jnp.where(lane == at + layers, total, now)

    span = windows[2] - windows[1]
    stops = KVH // 2

    def head_pair(i):
        loop(2 * i, 2 * i + 2, head)
        loop(
            windows[1] + lax.div(span * i, stops),
            windows[1] + lax.div(span * (i + 1), stops),
            send_blocks,
        )

    loop(0, stops, head_pair)

    pad = jnp.zeros((HD - rows, HD), jnp.float32)
    for r in range(REQS):
        for h in range(halves):
            start = (r * halves + h) * rows
            turned = jnp.concatenate([stat_cols[start : start + rows], pad], axis=0).T
            for g in range(KVH):
                chunk = (r * KVH + g) * halves + h
                stat[place_of(chunk // groups), chunk % groups] = turned[
                    g * STAT_ROWS : (g + 1) * STAT_ROWS
                ]

    def columns(factors):
        filler = jnp.zeros((HD - factors.shape[0], HD), jnp.float32)
        return jnp.concatenate([factors, filler], axis=0).T

    def join(acc_own, stat_own, acc_new, stat_new):
        for gi in range(groups):
            a, b = stat_own[gi], stat_new[gi]
            top = jnp.maximum(a[:layers], b[:layers])
            keep = jnp.exp(a[:layers] - top)
            add = jnp.exp(b[:layers] - top)
            total = a[layers : 2 * layers] * keep + b[layers : 2 * layers] * add
            filler = jnp.zeros((STAT_ROWS - 2 * layers, HD), jnp.float32)
            stat_own[gi] = jnp.concatenate([top, total, filler], axis=0)
            factor = columns(jnp.concatenate([keep, add], axis=0))
            for layer in range(layers):
                acc_own[gi, layer] = (
                    acc_own[gi, layer] * factor[:rows, layer : layer + 1]
                    + acc_new[gi, layer] * factor[:rows, layers + layer : layers + layer + 1]
                )

    def encode(acc_own, stat_own):
        for gi in range(groups):
            scales = jnp.zeros((rows, HD), jnp.float32)
            for layer in range(layers):
                value = acc_own[gi, layer]
                peak = jnp.max(jnp.abs(value), axis=1, keepdims=True)
                scale = jnp.maximum(peak, TINY) * (1.0 / LEVELS)
                steps_of = jnp.round(value / scale).astype(jnp.int32)
                coded[0, gi, layer] = steps_of.astype(jnp.int16)
                scales = jnp.where(lane == layer, scale, scales)
            turned = jnp.concatenate([scales, pad], axis=0).T
            stat_own[gi, 2 * layers : 3 * layers] = turned[:layers]

    def decode(at):
        for gi in range(groups):
            factor = columns(stat_in[at, gi, 2 * layers : 3 * layers])
            for layer in range(layers):
                value = coded_in[0, gi, layer].astype(jnp.int32).astype(jnp.float32)
                acc_in[at, gi, layer] = value * factor[:rows, layer : layer + 1]

    base = 0
    for stage in range(stages):
        half = n // 2 ** (stage + 1)
        bit = lax.rem(me // 2**stage, 2)
        partner = me + 2**stage * (1 - 2 * bit)
        keep, give = base + bit * half, base + (1 - bit) * half
        at = n - 2 * half
        last = stage == stages - 1
        if last:
            encode(acc.at[give], stat.at[give])
        sums = (coded, coded_in) if last else (acc.at[pl.ds(give, half)], acc_in.at[pl.ds(at, half)])
        notes = (stat.at[pl.ds(give, half)], stat_in.at[pl.ds(at, half)])
        copies = [
            send(src, dst, pair_send.at[i, stage], pair_recv.at[i, stage], partner)
            for i, (src, dst) in enumerate((notes, sums))
        ]
        for copy in copies:
            copy.start()
        loop(windows[2 + stage], windows[3 + stage], send_blocks)
        for copy in copies:
            copy.wait()
        if last:
            decode(at)
        loop(
            0,
            half,
            lambda i, keep=keep, at=at: join(
                acc.at[keep + i], stat.at[keep + i], acc_in.at[at + i], stat_in.at[at + i]
            ),
        )
        base = keep

    share = rows // result.shape[0]
    for gi in range(groups):
        totals = stat[base, gi, layers : 2 * layers]
        factor = columns(1.0 / totals)
        for layer in range(layers):
            out = acc[base, gi, layer] * factor[:rows, layer : layer + 1]
            for step in range(result.shape[0]):
                result[step, layer, gi * share : (gi + 1) * share, :] = out[
                    step * share : (step + 1) * share
                ]

    own_copy.wait()
    loop(1, n, lambda k: block_copy(k).wait())


def exchange(n, cap, lengths, *arrays):
    cache, queries = arrays[:2]
    steps, layers, requests, _ = queries.shape
    share = requests * KVH * QPG // n
    groups = max(share // QPG, 1)
    halves = max(QPG // share, 1)
    heads = QPG // halves
    rows = steps * heads
    fresh_pad = -(-steps * requests // 16) * 16
    stages = n.bit_length() - 1
    block = cache.shape[1:]
    per_dev, block_len = cache.shape[0], cache.shape[3]
    slots = -(-n * cap // HD) * HD
    piece = (groups, layers, rows, HD)
    note = (groups, STAT_ROWS, HD)
    vmem = pl.BlockSpec(memory_space=pltpu.VMEM)
    smem = pl.BlockSpec(memory_space=pltpu.SMEM)
    hbm = pl.BlockSpec(memory_space=pl.ANY)
    dma = pltpu.SemaphoreType.DMA
    f32 = jnp.float32
    return pl.pallas_call(
        functools.partial(exchange_kernel, n, groups, halves),
        out_shape=(
            jax.ShapeDtypeStruct((n, cap) + block, cache.dtype),
            jax.ShapeDtypeStruct((steps, layers, share, HD), f32),
            jax.ShapeDtypeStruct((1, per_dev), jnp.int32),
        ),
        in_specs=[smem] + [pl.BlockSpec(memory_space=pltpu.HBM)] * len(arrays),
        out_specs=(hbm, vmem, vmem),
        scratch_shapes=[pltpu.VMEM(array.shape, array.dtype) for array in arrays]
        + [
            pltpu.VMEM((n, cap) + block, cache.dtype),
            pltpu.VMEM((1, slots), jnp.int32),
            pltpu.SMEM((1, slots), jnp.int32),
            pltpu.VMEM((1, per_dev * block_len), jnp.int32),
            pltpu.VMEM((2, layers, fresh_pad, KVH * HD), cache.dtype),
            pltpu.VMEM((requests * halves * rows, fresh_pad), f32),
            pltpu.VMEM((n,) + piece, f32),
            pltpu.VMEM((n - 1,) + piece, f32),
            pltpu.VMEM((1,) + piece, jnp.int16),
            pltpu.VMEM((1,) + piece, jnp.int16),
            pltpu.VMEM((n,) + note, f32),
            pltpu.VMEM((n - 1,) + note, f32),
            pltpu.VMEM((requests * halves * rows, HD), f32),
            dma((n,)),
            dma((n,)),
            dma((2, stages)),
            dma((2, stages)),
            dma((8,)),
        ],
        compiler_params=pltpu.CompilerParams(
            collective_id=0, has_side_effects=True, vmem_limit_bytes=60 * 1024 * 1024
        ),
        name="exchange",
    )(lengths, *arrays)


def local(src_cache, src_blocks, dst_blocks, ctx_lengths, queries, new_keys, new_values):
    n = lax.axis_size("ctx")
    cap = (src_cache.shape[0] + n - 1) // n
    tables = [blocks.reshape(1, -1) for blocks in (src_blocks, dst_blocks)]
    arrived, attn, take_index = exchange(
        n, cap, ctx_lengths, src_cache, queries, new_keys, new_values, *tables
    )
    return place(arrived, attn, take_index)


def solution(mesh):
    in_specs = (
        P(("groups", "ctx"), None, None, None, None),
        P("groups"),
        P("groups"),
        P("groups"),
        P(None, None, "groups", None),
        P(None, None, "groups", None),
        P(None, None, "groups", None),
    )
    out_specs = (
        P(("groups", "ctx"), None, None, None, None),
        P(None, None, ("groups", "ctx"), None),
    )
    return jax.shard_map(local, mesh=mesh, in_specs=in_specs, out_specs=out_specs, check_vma=False)
```
